32 devices in a mesh: seq: 8 (over y, x, core), tp: 4 (over z).
Axes of the slice: x: 2, y: 2, z: 4, core: 2. Of those that a mesh axis runs over, the one named last changes fastest.
Arguments:
- hidden: bfloat16 [6144, 8192], P('seq', 'tp'), may hold values from -6 to 6
- cotangent: bfloat16 [6144, 8192], P('seq', 'tp'), may hold values from -0.59765625 to 0.59765625
- router_gate: bfloat16 [6144], P('seq'), may hold values from 0.25 to 1
- recursion_depth: int32 [6144], P('seq'), may hold values from 1 to 4
- live_counts: int32 [8], replicated, may hold values from 0 to 768, as said below
- out_weight: bfloat16 [8192, 8192], P(None, 'tp'), may hold values from -0.0625 to 0.0625
- adapter_down: bfloat16 [8192, 1024], P('tp', 'seq'), may hold values from -0.0625 to 0.0625
- adapter_up: bfloat16 [1024, 8192], P('seq', 'tp'), may hold values from -0.375 to 0.375
Outputs:
- hidden_grad: float32 [6144, 8192], P('seq', 'tp')
- gate_grad: float32 [6144], P('seq')
- weight_grad: float32 [8192, 8192], P('seq', 'tp')
- down_grad: float32 [1024, 8192], P('seq', 'tp')
- up_grad: float32 [1024, 8192], P('seq', 'tp')
The draws below stay inside these ranges and needn't reach their ends.
Inputs may be any that keep to these rules, and one draw needn't show every extreme that they name: `live_counts`: each entry is a multiple of 128; the entries sum to 3072; the largest entry equals 768. Rows at or past an index's count are not live.
All inputs are finite; a program needn't handle non-finite values.
Results may differ from the reference program's by a relative error of at most 0.0055.
Values may be sent and summed in bfloat16 or wider, within the bound.
No kernel may reach another device: no remote copies, remote signals or barrier semaphores. Data moves between devices by JAX's collectives and lax.ppermute only.
A program may use at most 256 MiB of HBM per device.

```python
import jax
import jax.numpy as jnp

D = 8192
RANK = 256
NREC = 4
BLOCK = 128
BAL = 384
CAP = 768
SLOTS = 6144
N_SEQ = 8


def draw_live_counts(key, part):
    block_mean = BAL // BLOCK
    carried = jax.random.randint(jax.random.fold_in(key, 11), (N_SEQ,), 0, block_mean + 1)
    carried = carried.at[0].set(block_mean).at[N_SEQ - 1].set(0)
    in_blocks = block_mean + carried - jnp.roll(carried, 1)
    placing = jax.random.permutation(jax.random.fold_in(key, 12), N_SEQ)
    placed = jnp.zeros((N_SEQ,), jnp.int32).at[placing].set(in_blocks.astype(jnp.int32))
    return (placed * BLOCK).astype(jnp.int32)


def touch_ends(drawn, rng, low, top_value):
    longest = drawn.shape.index(max(drawn.shape))
    spots = []
    for shift in (0, 1):
        where = [jax.random.randint(jax.random.fold_in(rng, axis), (), 0, length) for axis, length in enumerate(drawn.shape)]
        where[longest] = (where[longest] + shift) % drawn.shape[longest]
        spots.append(tuple(where))
    return drawn.at[spots[0]].set(low).at[spots[1]].set(top_value)


def block_levels(rng, shape, pieces, smallest, high):
    level, own = 1.0, jax.random.fold_in(rng, 6)
    for axis_at, shards_of in pieces:
        steps = jnp.exp(jax.random.uniform(jax.random.fold_in(own, axis_at), (shards_of,), jnp.float32, smallest / len(pieces), high / len(pieces)))
        level = level * jnp.repeat(steps, shape[axis_at] // shards_of).reshape([-1 if axis == axis_at else 1 for axis in range(len(shape))])
    return level


def bell_draw(own_key, extent, scale, limit, cuts=(), held_as=jnp.bfloat16):
    array = scale * jax.random.normal(own_key, extent, jnp.float32)
    if cuts:
        array = array * block_levels(own_key, extent, cuts, -0.22, 0.18)
    return jnp.clip(array, -limit, limit).astype(held_as)


def setup_inputs(seed: int = 0) -> dict:
    key_list = jax.random.split(jax.random.key(seed), 9)
    hidden = bell_draw(key_list[0], (SLOTS, D), 1.0, 6.0, ((0, 8), (1, 4)))
    cotangent = bell_draw(key_list[1], (SLOTS, D), 0.1, 0.59765625, ((0, 8), (1, 4)))
    router_gate = jnp.clip(0.25 + 0.75 * jax.random.uniform(key_list[2], (SLOTS,), jnp.float32) ** block_levels(key_list[2], (SLOTS,), ((0, 8),), -0.2, 0.2), 0.25, 1.0).astype(jnp.bfloat16)
    recursion_depth = touch_ends(jax.random.randint(key_list[3], (SLOTS,), 1, 5), jax.random.fold_in(key_list[3], 1), 1, 4).astype(jnp.int32)
    live_counts = draw_live_counts(jax.random.fold_in(key_list[8], 71), 0)
    out_weight = bell_draw(key_list[5], (D, D), D ** -0.5, 0.0625, ((1, 4),))
    adapter_down = bell_draw(key_list[6], (D, NREC * RANK), D ** -0.5, 0.0625, ((0, 4), (1, 8)))
    adapter_up = bell_draw(key_list[7], (NREC * RANK, D), RANK ** -0.5, 0.375, ((0, 8), (1, 4)))
    return dict(hidden=hidden, cotangent=cotangent, router_gate=router_gate, recursion_depth=recursion_depth, live_counts=live_counts, out_weight=out_weight, adapter_down=adapter_down, adapter_up=adapter_up)


adapter_scale = 0.5


def reference(hidden, cotangent, router_gate, recursion_depth, live_counts, out_weight, adapter_down, adapter_up):
    total_live = N_SEQ * BAL
    finish = jnp.cumsum(live_counts).astype(jnp.int32)
    starts_at = (finish - live_counts).astype(jnp.int32)
    rank_slots = jnp.arange(total_live, dtype=jnp.int32)
    source = jnp.sum((finish[None, :] <= rank_slots[:, None]).astype(jnp.int32), axis=1).astype(jnp.int32)
    shard_ids = jnp.arange(N_SEQ, dtype=jnp.int32)
    begin_at = jnp.sum(jnp.where(source[:, None] == shard_ids[None, :], starts_at[None, :], 0), axis=1).astype(jnp.int32)
    row_index = (source * CAP + rank_slots - begin_at).astype(jnp.int32)
    rows_h = jnp.take(hidden, row_index, axis=0)
    rows_dy = jnp.take(cotangent, row_index, axis=0)
    gate_rows = jnp.take(router_gate, row_index).astype(jnp.float32)
    depths = jnp.take(recursion_depth, row_index).astype(jnp.int32)
    levels = jnp.arange(1, NREC + 1, dtype=jnp.int32)
    selector = (depths[:, None] == levels[None, :]).astype(jnp.float32)
    down_all = jnp.dot(rows_h, adapter_down, preferred_element_type=jnp.float32)
    down_proj = jnp.sum(down_all.reshape(total_live, NREC, RANK) * selector[:, :, None], axis=1)
    up_all = jnp.dot(rows_dy, adapter_up.T, preferred_element_type=jnp.float32)
    up_back = adapter_scale * jnp.sum(up_all.reshape(total_live, NREC, RANK) * selector[:, :, None], axis=1)
    wide_back = (selector[:, :, None] * up_back[:, None, :]).reshape(total_live, NREC * RANK)
    wide_down = (selector[:, :, None] * down_proj[:, None, :]).reshape(total_live, NREC * RANK)
    pre_grad = jnp.dot(rows_dy, out_weight, preferred_element_type=jnp.float32)
    pre_grad = pre_grad + jnp.dot(wide_back.astype(jnp.bfloat16), adapter_down.T, preferred_element_type=jnp.float32)
    row_grad = gate_rows[:, None] * pre_grad
    gate_row = jnp.sum(rows_h.astype(jnp.float32) * pre_grad, axis=1)
    hidden_grad = jnp.zeros((N_SEQ * CAP, D), jnp.float32).at[row_index].set(row_grad)
    gate_grad = jnp.zeros((N_SEQ * CAP,), jnp.float32).at[row_index].set(gate_row)
    gated_dy = (gate_rows[:, None] * rows_dy.astype(jnp.float32)).astype(jnp.bfloat16)
    weight_grad = jnp.dot(gated_dy.T, rows_h, preferred_element_type=jnp.float32)
    back_gated = (gate_rows[:, None] * wide_back).astype(jnp.bfloat16)
    down_grad = jnp.dot(back_gated.T, rows_h, preferred_element_type=jnp.float32)
    down_gated = (gate_rows[:, None] * adapter_scale * wide_down).astype(jnp.bfloat16)
    up_grad = jnp.dot(down_gated.T, rows_dy, preferred_element_type=jnp.float32)
    return hidden_grad, gate_grad, weight_grad, down_grad, up_grad
```

```python
import jax
import jax.numpy as jnp
from jax import lax
from jax.sharding import PartitionSpec as P

NREC = 4
CHUNKS = 4
adapter_scale = 0.5
contract_rows = (((0,), (0,)), ((), ()))
contract_last = (((1,), (1,)), ((), ()))
f32 = jnp.float32
bf16 = jnp.bfloat16


def dot_rows(a, b):
    return lax.dot_general(a, b, contract_rows, preferred_element_type=f32)


def flip(value, bit):
    size = lax.axis_size("seq")
    return lax.ppermute(value, "seq", [(i, i ^ (1 << bit)) for i in range(size)])


def after(value, earlier):
    return lax.optimization_barrier((value, earlier))[0]


def masks_of(bits):
    masks = [0]
    for bit in bits:
        masks = masks + [m | (1 << bit) for m in masks]
    return masks


def gather_seq(block, bits):
    size, me = lax.axis_size("seq"), lax.axis_index("seq")
    have = block[None]
    for bit in bits:
        have = jnp.concatenate([have, flip(have, bit)], axis=0)
    place = [0] * size
    for at, mask in enumerate(masks_of(bits)):
        place[mask] = at
    order = jnp.take(jnp.array(place, jnp.int32), me ^ jnp.arange(size, dtype=jnp.int32))
    have = jnp.take(have, order, axis=0, mode="clip")
    return have.reshape(size * block.shape[0], block.shape[1])


def gather_line(own, earlier):
    size, me = lax.axis_size("tp"), lax.axis_index("tp")
    if earlier is not None:
        own = after(own, earlier)
    ups, downs = [own], [own]
    for k in range(1, size):
        ups.append(lax.ppermute(ups[-1], "tp", [(i, i + 1) for i in range(k - 1, size - 1)]))
        downs.append(lax.ppermute(downs[-1], "tp", [(i, i - 1) for i in range(1, size - k + 1)]))
    line = jnp.concatenate(ups[:0:-1] + [own] + downs[1:], axis=1)
    width = own.shape[1]
    return lax.dynamic_slice_in_dim(line, (size - 1 - me) * width, size * width, axis=1), (ups[1], downs[1])


def sum_line(part):
    size = lax.axis_size("tp")
    below = above = jnp.zeros_like(part)
    for k in range(1, size):
        below = below + lax.ppermute((part + below).astype(bf16), "tp", [(k - 1, k)]).astype(f32)
        above = above + lax.ppermute((part + above).astype(bf16), "tp", [(size - k, size - k - 1)]).astype(f32)
    return part + below + above


def local(
    hidden,
    cotangent,
    router_gate,
    recursion_depth,
    live_counts,
    out_weight,
    adapter_down,
    adapter_up,
):
    shards, planes = lax.axis_size("seq"), lax.axis_size("tp")
    me = lax.axis_index("seq")
    core, chip = me & 1, me >> 1
    chips = shards // 2
    chip_bits = list(range(1, shards.bit_length() - 1))
    rows, width = hidden.shape
    own_outs = width * planes // shards
    per_block = width // own_outs
    cut = own_outs // CHUNKS
    rank_rows = adapter_up.shape[0]
    rank = rank_rows * shards // NREC

    live = jnp.arange(rows, dtype=jnp.int32) < lax.dynamic_index_in_dim(live_counts, me, 0, False)
    dy = jnp.where(live[:, None], cotangent, jnp.zeros((), bf16))
    small = jnp.stack([router_gate, recursion_depth.astype(bf16)])
    small_both = jnp.concatenate([small, flip(small, 0)], axis=1)
    gate_both, depth_both = small_both[0].astype(f32), small_both[1].astype(f32)
    gate, depth = router_gate.astype(f32), recursion_depth.astype(f32)

    dy_cut = dy.reshape(rows, per_block, CHUNKS, cut)
    gathered, earlier = [], None
    for j in range(CHUNKS):
        piece = dy_cut[:, :, j].reshape(rows, per_block * cut)
        whole, earlier = gather_line(piece, earlier)
        gathered.append(whole)

    hidden_both = jnp.concatenate([hidden, flip(hidden, 0)], axis=0)
    dy_both = jnp.concatenate([dy, flip(dy, 0)], axis=0)
    gated_hidden = (gate_both[:, None] * hidden_both.astype(f32)).astype(bf16)

    downs_t = gather_seq(adapter_down.T, chip_bits + [0])
    ups = gather_seq(adapter_up, chip_bits[::-1] + [0])

    def select(wide):
        return sum(
            jnp.where((depth == d + 1)[:, None], wide[:, d * rank : (d + 1) * rank], 0.0)
            for d in range(NREC)
        )

    down_part = select(lax.dot_general(hidden, downs_t, contract_last, preferred_element_type=f32))
    up_part = select(lax.dot_general(dy, ups, contract_last, preferred_element_type=f32))
    summed = sum_line(jnp.concatenate([down_part, up_part], axis=1))
    down, up = summed[:, :rank], adapter_scale * summed[:, rank:]
    wide_back = jnp.concatenate(
        [jnp.where((depth == d + 1)[:, None], up, 0.0) for d in range(NREC)], axis=1
    ).astype(bf16)
    grads = jnp.concatenate([gate[:, None] * up, gate[:, None] * adapter_scale * down], axis=1).astype(bf16)
    grads_both = jnp.concatenate([grads, flip(grads, 0)], axis=0)

    half = width // 2
    order = [g ^ (g >> 1) for g in range(chips)]

    def columns(values, size, wanted):
        spots = [order.index(m) for m in wanted]
        lo, hi = min(spots), max(spots)
        if hi - lo + 1 == len(spots):
            return values[:, lo * size : (hi + 1) * size], [order[i] for i in range(lo, hi + 1)]
        return jnp.concatenate([values[:, i * size : (i + 1) * size] for i in spots], axis=1), wanted

    def scatter(left, right, size, bits):
        everything = list(range(chips))
        first = bits[0] - 1
        away, away_at = columns(left, size, [m for m in everything if m >> first & 1])
        stay, stay_at = columns(left, size, [m for m in everything if not m >> first & 1])
        sent = flip(dot_rows(away, right).astype(bf16), bits[0])
        kept = dot_rows(stay, right)
        sums = {}
        for i, m in enumerate(stay_at):
            at = away_at.index(m | 1 << first)
            sums[m] = kept[i * size : (i + 1) * size] + sent[at * size : (at + 1) * size].astype(f32)
        for bit in bits[1:]:
            b = 1 << (bit - 1)
            moving = [m for m in sums if m & b]
            sent = flip(jnp.concatenate([sums[m] for m in moving], axis=0).astype(bf16), bit)
            for i, m in enumerate(moving):
                sums[m ^ b] = sums[m ^ b] + sent[i * size : (i + 1) * size].astype(f32)
                del sums[m]
        return sums[0]

    def rank_columns(values):
        parts = []
        for m in order:
            first = ((chip ^ m) * 2 + core) * rank_rows
            part = lax.dynamic_slice_in_dim(values, first % rank, rank_rows, axis=1)
            parts.append(jnp.where((depth_both == (first // rank + 1).astype(f32))[:, None], part, jnp.zeros((), bf16)))
        return jnp.concatenate(parts, axis=1)

    down_grad = scatter(rank_columns(grads_both[:, :rank]), hidden_both, rank_rows, chip_bits)
    up_grad = scatter(rank_columns(grads_both[:, rank:]), dy_both, rank_rows, chip_bits[::-1])

    weight_cut = out_weight.reshape(shards, CHUNKS, cut, width)
    pre = None
    weight_rows = []
    for j in range(CHUNKS):
        whole = gathered[j]

        def of_core(which):
            return jnp.concatenate(
                [
                    lax.dynamic_slice_in_dim(whole, ((chip ^ m) * 2 + which) * cut, cut, axis=1)
                    for m in order
                ],
                axis=1,
            )

        left = jnp.concatenate([of_core(core), flip(of_core(1 - core), 0)], axis=0)
        weight_rows.append(
            jnp.concatenate(
                [
                    scatter(left, gated_hidden[:, :half], cut, chip_bits),
                    scatter(left, gated_hidden[:, half:], cut, chip_bits[::-1]),
                ],
                axis=1,
            )
        )
        term = jnp.dot(whole, weight_cut[:, j].reshape(shards * cut, width), preferred_element_type=f32)
        pre = term if pre is None else pre + term
    weight_grad = jnp.concatenate(weight_rows, axis=0)

    pre = pre + jnp.dot(wide_back, downs_t, preferred_element_type=f32)
    hidden_grad = gate[:, None] * pre
    gate_grad = lax.psum(jnp.sum(hidden.astype(f32) * pre, axis=1), "tp")
    return (hidden_grad, gate_grad, weight_grad, down_grad, up_grad)


def solution(mesh):
    in_specs = (
        P("seq", "tp"),
        P("seq", "tp"),
        P("seq"),
        P("seq"),
        P(),
        P(None, "tp"),
        P("tp", "seq"),
        P("seq", "tp"),
    )
    out_specs = (P("seq", "tp"), P("seq"), P("seq", "tp"), P("seq", "tp"), P("seq", "tp"))
    return jax.shard_map(local, mesh=mesh, in_specs=in_specs, out_specs=out_specs, check_vma=False)
```

```python
import jax
import jax.numpy as jnp
from jax import lax
from jax.experimental import pallas as pl
from jax.experimental.pallas import tpu as pltpu
from jax.sharding import PartitionSpec as P

NREC = 4
LANES = 128
adapter_scale = 0.5
contract_rows = (((0,), (0,)), ((), ()))
contract_last = (((1,), (1,)), ((), ()))
f32 = jnp.float32
bf16 = jnp.bfloat16


def dot_rows(pairs):
    return sum(
        lax.dot_general(a, b, contract_rows, preferred_element_type=f32) for a, b in pairs
    )


def flip(value, bit):
    size = lax.axis_size("seq")
    return lax.ppermute(value, "seq", [(i, i ^ (1 << bit)) for i in range(size)])


def run(streams):
    results = [None] * len(streams)
    alive = dict(enumerate(streams))
    while alive:
        made = {}
        for i in list(alive):
            try:
                made[i] = alive[i].send(results[i])
            except StopIteration:
                del alive[i]
                results[i] = None
        held = lax.optimization_barrier(made)
        for i, values in held.items():
            results[i] = values


def chunk_sizes(units):
    quarter = max(1, units // 4)
    return [quarter] * (units // quarter)


def add_products(total, terms, closing=None):
    rows, width = terms[0][0].shape[0], terms[0][1].shape[2]
    wide = min(width, 512)
    tiles = width // wide

    def kernel(*refs):
        refs = list(refs)
        done = refs.pop(0)[...] if total is not None else None
        for left, right, _, cut in terms:
            left_ref, right_ref = refs.pop(0), refs.pop(0)
            term = jnp.dot(
                left_ref[...],
                right_ref[...].reshape(right.shape[0] * cut, wide),
                preferred_element_type=f32,
            )
            done = term if done is None else done + term
        if closing is not None:
            scale_ref, hidden_ref, out_ref, sum_ref = refs
            part = jnp.sum(hidden_ref[...].astype(f32) * done, axis=1, keepdims=True)
            first = pl.program_id(0) == 0

            @pl.when(first)
            def _():
                sum_ref[...] = part

            @pl.when(jnp.logical_not(first))
            def _():
                sum_ref[...] += part

            done = scale_ref[...] * done
        else:
            (out_ref,) = refs
        out_ref[...] = done

    in_specs, operands = [], []
    tile = pl.BlockSpec((rows, wide), lambda n: (0, n))
    column = pl.BlockSpec((rows, 1), lambda n: (0, 0))
    if total is not None:
        operands.append(total)
        in_specs.append(tile)
    for left, right, start, cut in terms:
        groups = right.shape[0]
        operands += [left, right]
        in_specs += [
            pl.BlockSpec((rows, groups * cut), lambda n: (0, 0)),
            pl.BlockSpec(
                (pl.Element(groups), pl.Element(cut), pl.Element(wide)),
                lambda n, start=start: (0, start, n * wide),
            ),
        ]
    out_shape, out_specs = [jax.ShapeDtypeStruct((rows, width), f32)], [tile]
    if closing is not None:
        operands += [closing[0][:, None], closing[1]]
        in_specs += [column, tile]
        out_shape.append(jax.ShapeDtypeStruct((rows, 1), f32))
        out_specs.append(column)
    return pl.pallas_call(
        kernel,
        grid=(tiles,),
        in_specs=in_specs,
        out_specs=out_specs,
        out_shape=out_shape,
        input_output_aliases={0: 0} if total is not None else {},
        compiler_params=pltpu.CompilerParams(vmem_limit_bytes=48 * 2**20),
        cost_estimate=pl.CostEstimate(flops=0, bytes_accessed=0, transcendentals=0),
    )(*operands)


def masks_of(bits):
    masks = [0]
    for bit in bits:
        masks = masks + [m | (1 << bit) for m in masks]
    return masks


def column_products(lefts, rights, cut, picks, moving, added=None):
    depth, columns = lefts[0].shape
    half = rights[0].shape[1] // 2
    pairs = len(lefts)
    wide = min(half, 512)
    per = half // wide
    count = len(picks[0])
    kinds = [(moving, bf16)] * (moving > 0) + [(count - moving, f32)] * (count > moving)

    def kernel(*refs):
        left_refs, right_refs, refs = refs[:pairs], refs[pairs : 2 * pairs], refs[2 * pairs :]
        added_refs = refs[:2] if added is not None else None
        out_refs = refs[2 if added is not None else 0 :]
        for h in range(2):

            @pl.when(pl.program_id(0) // per == h)
            def _():
                chosen = [
                    jnp.concatenate(
                        [left_ref[:, p * cut : (p + 1) * cut] for p in picks[h]], axis=1
                    )
                    for left_ref in left_refs
                ]
                term = dot_rows([(a, ref[...]) for a, ref in zip(chosen, right_refs)])
                if added_refs is not None:
                    term = term + added_refs[h][...].astype(f32)
                first = 0
                for i, (blocks, kind) in enumerate(kinds):
                    out_refs[2 * i + h][...] = term[first : first + blocks * cut].astype(kind)
                    first += blocks * cut

    def halves(blocks):
        return [
            pl.BlockSpec((blocks * cut, wide), lambda n: (0, jnp.minimum(n, per - 1))),
            pl.BlockSpec((blocks * cut, wide), lambda n: (0, jnp.maximum(n - per, 0))),
        ]

    return pl.pallas_call(
        kernel,
        grid=(2 * per,),
        in_specs=[pl.BlockSpec((depth, columns), lambda n: (0, 0))] * pairs
        + [pl.BlockSpec((depth, wide), lambda n: (0, n))] * pairs
        + (halves(count) if added is not None else []),
        out_specs=[spec for blocks, _ in kinds for spec in halves(blocks)],
        out_shape=[
            jax.ShapeDtypeStruct((blocks * cut, half), kind)
            for blocks, kind in kinds
            for _ in range(2)
        ],
        compiler_params=pltpu.CompilerParams(vmem_limit_bytes=40 * 2**20),
        cost_estimate=pl.CostEstimate(flops=0, bytes_accessed=0, transcendentals=0),
    )(*lefts, *rights, *(added if added is not None else ()))


def lay_out(ups, downs, cut, order):
    planes, chips = lax.axis_size("tp"), len(order)
    rows, piece = ups[0].shape
    me = lax.axis_index("seq")
    where = jnp.stack([lax.axis_index("tp"), me >> 1, me & 1]).astype(jnp.int32)

    def kernel(where_ref, *refs):
        parts, (whole_ref, mine_ref, theirs_ref, whole, in_sem, out_sem) = refs[:-6], refs[-6:]
        plane, chip, core = where_ref[0], where_ref[1], where_ref[2]

        def place(part, b):
            return pltpu.make_async_copy(part, whole.at[:, b * piece : (b + 1) * piece], in_sem)

        for at, part in enumerate(parts):
            for b in range(planes):
                if 0 <= b - at + planes - 1 < planes:

                    @pl.when(plane == b - at + planes - 1)
                    def _():
                        place(part, b).start()

        for b in range(planes):
            place(parts[0], b).wait()
        copies = [pltpu.make_async_copy(whole, whole_ref, out_sem.at[0])]
        for at, mask in enumerate(order):
            for which, ref in ((core, mine_ref), (1 - core, theirs_ref)):
                column = pl.multiple_of(((chip ^ mask) * 2 + which) * cut, LANES)
                copies.append(
                    pltpu.make_async_copy(
                        whole.at[:, pl.ds(column, cut)],
                        ref.at[:, at * cut : (at + 1) * cut],
                        out_sem.at[len(copies)],
                    )
                )
        for copy in copies:
            copy.start()
        for copy in copies:
            copy.wait()

    parts = ups[:0:-1] + downs
    anywhere = pl.BlockSpec(memory_space=pl.ANY)
    return pl.pallas_call(
        kernel,
        in_specs=[pl.BlockSpec(memory_space=pltpu.SMEM)] + [anywhere] * len(parts),
        out_specs=[anywhere] * 3,
        out_shape=[
            jax.ShapeDtypeStruct((rows, planes * piece), bf16),
            jax.ShapeDtypeStruct((rows, chips * cut), bf16),
            jax.ShapeDtypeStruct((rows, chips * cut), bf16),
        ],
        scratch_shapes=[
            pltpu.VMEM((rows, planes * piece), bf16),
            pltpu.SemaphoreType.DMA,
            pltpu.SemaphoreType.DMA((1 + 2 * chips,)),
        ],
        compiler_params=pltpu.CompilerParams(vmem_limit_bytes=16 * 2**20),
        cost_estimate=pl.CostEstimate(flops=0, bytes_accessed=0, transcendentals=0),
    )(where, *parts)


def local(
    hidden,
    cotangent,
    router_gate,
    recursion_depth,
    live_counts,
    out_weight,
    adapter_down,
    adapter_up,
):
    shards, planes = lax.axis_size("seq"), lax.axis_size("tp")
    me, plane = lax.axis_index("seq"), lax.axis_index("tp")
    core, chip = me & 1, me >> 1
    chips = shards // 2
    chip_bits = list(range(1, shards.bit_length() - 1))
    rows, width = hidden.shape
    own_outs = width * planes // shards
    per_block = width // own_outs
    rank_rows = adapter_up.shape[0]
    rank = rank_rows * shards // NREC
    half = width // 2
    order = [i ^ (i >> 1) for i in range(chips)]
    cuts, first = [], 0
    for share in chunk_sizes(own_outs // LANES):
        cuts.append((first, share * LANES))
        first += share * LANES

    live = jnp.arange(rows, dtype=jnp.int32) < lax.dynamic_index_in_dim(live_counts, me, 0, False)
    dy = jnp.where(live[:, None], cotangent, jnp.zeros((), bf16))
    gate, depth = router_gate.astype(f32), recursion_depth.astype(f32)
    state = {"whole": {}, "step": 0, "hold": False, "weight": jnp.zeros((own_outs, width), f32)}

    pieces = [
        jnp.concatenate(
            [dy[:, i * own_outs + start : i * own_outs + start + cut] for i in range(per_block)],
            axis=1,
        )
        for start, cut in cuts
    ]

    def line():
        later = pieces
        for j in range(len(cuts)):
            ups, downs = [later[0]], [later[0]]
            later = later[1:]
            for k in range(1, planes):
                if state["hold"]:
                    state["hold"] = False
                    later = yield later
                state["step"] = k
                up = lax.ppermute(ups[-1], "tp", [(i, i + 1) for i in range(k - 1, planes - 1)])
                down = lax.ppermute(downs[-1], "tp", [(i, i - 1) for i in range(1, planes - k + 1)])
                up, down, later = yield (up, down, later)
                ups.append(up)
                downs.append(down)
            state["whole"][j] = (ups, downs)
        state["step"] = 0

    def columns(values, size, wanted):
        spots = [order.index(m) for m in wanted]
        lo, hi = min(spots), max(spots)
        if hi - lo + 1 == len(spots):
            return values[:, lo * size : (hi + 1) * size], [order[i] for i in range(lo, hi + 1)]
        return jnp.concatenate([values[:, i * size : (i + 1) * size] for i in spots], axis=1), wanted

    def scatter(jobs, size):
        sums, sent = [], []
        for pairs, bits in jobs:
            first_bit = bits[0] - 1
            away = [m for m in range(chips) if m >> first_bit & 1]
            away_pairs = [(columns(a, size, away)[0], b) for a, b in pairs]
            sent.append((dot_rows(away_pairs).astype(bf16), columns(pairs[0][0], size, away)[1]))
            sums.append({})
        made = yield [values for values, _ in sent]
        while state["step"] > 1:
            made = yield made
        made = yield [flip(values, bits[0]) for values, (_, bits) in zip(made, jobs)]
        for step in range(1, len(chip_bits) + 1):
            sent_before, sent = sent, []
            for total, got, (_, at), (pairs, bits) in zip(sums, made, sent_before, jobs):
                before = 1 << (bits[step - 1] - 1)
                arrived = {
                    m ^ before: got[i * size : (i + 1) * size].astype(f32) for i, m in enumerate(at)
                }
                for m in arrived:
                    own = total.pop(m, None)
                    if own is None:
                        own = dot_rows([(columns(a, size, [m])[0], b) for a, b in pairs])
                    total[m] = own + arrived[m]
                if step < len(chip_bits):
                    moving = [m for m in total if m >> (bits[step] - 1) & 1]
                    sent.append(([total.pop(m).astype(bf16) for m in moving], moving))
            if step < len(chip_bits):
                made = [jnp.concatenate(values, axis=0) for values, _ in sent]
                made, sums = yield (made, sums)
                while state["step"] > 1:
                    made = yield made
                made = yield [flip(values, bits[step]) for values, (_, bits) in zip(made, jobs)]
        return [total[0] for total in sums]

    def weights():
        small = jnp.stack([router_gate, recursion_depth.astype(bf16)])
        other_small, now = yield (flip(small, 0), hidden)
        other_hidden = flip(now, 0)
        gated = (gate[:, None] * hidden.astype(f32)).astype(bf16)
        other_hidden, gated, now = yield (other_hidden, gated, dy)
        other_dy = flip(now, 0)
        other_gate, other_depth = other_small[0].astype(f32), other_small[1].astype(f32)
        other_gated = (other_gate[:, None] * other_hidden.astype(f32)).astype(bf16)
        state["other"] = yield (other_hidden, other_dy, other_depth)
        state["gated"] = (gated, other_gated)

    def weight_chunk(j):
        start, cut = cuts[j]
        while j not in state["whole"]:
            yield ()
        whole, mine, theirs = lay_out(*state["whole"][j], cut, order)
        left = (mine, flip(theirs, 0))
        if j == 0:
            whole, left = yield (whole, left)
        state["terms"].append(whole)
        paths = [[bit - 1 for bit in chip_bits], [bit - 1 for bit in chip_bits[::-1]]]
        stay = []
        for bits in paths:
            kept = [m for m in range(chips) if not m >> bits[0] & 1]
            if len(bits) > 1:
                gone = [m for m in kept if m >> bits[1] & 1]
                kept = gone + [m ^ 1 << bits[1] for m in gone]
            stay.append(kept)
        away = [[m | 1 << bits[0] for m in kept] for kept, bits in zip(stay, paths)]
        spots = [[order.index(m) for m in kept] for kept in away]
        sent = column_products(left, state["gated"], cut, spots, len(spots[0]))
        sent, left = yield (sent, left)
        got = yield [flip(values, bits[0] + 1) for values, bits in zip(sent, paths)]
        spots = [[order.index(m) for m in kept] for kept in stay]
        parts = column_products(left, state["gated"], cut, spots, chips // 4, got)
        moved, rest = (parts[:2], parts[2:]) if len(parts) > 2 else (None, parts)
        for step in range(1, len(chip_bits)):
            got, rest = yield ([flip(values, bits[step] + 1) for values, bits in zip(moved, paths)], rest)
            rest = [own + new.astype(f32) for own, new in zip(rest, got)]
            stay = [kept[len(kept) // 2 :] for kept in stay]
            if step + 1 < len(chip_bits):
                moved, after = [], []
                for total, kept, bits in zip(rest, stay, paths):
                    place = {m: total[i * cut : (i + 1) * cut] for i, m in enumerate(kept)}
                    gone = [m for m in kept if m >> bits[step + 1] & 1]
                    moved.append(jnp.concatenate([place[m].astype(bf16) for m in gone], axis=0))
                    after.append([place[m ^ 1 << bits[step + 1]] for m in gone])
                    kept[:] = gone + [m ^ 1 << bits[step + 1] for m in gone]
                rest = [jnp.concatenate(values, axis=0) for values in after]
        state["weight"] = lax.dynamic_update_slice(
            state["weight"], jnp.concatenate(rest, axis=1), (start, 0)
        )

    state["terms"] = []

    def rows_of_pre():
        weight_blocks = out_weight.reshape(shards, own_outs, width)

        def term(j):
            return (state["terms"][j], weight_blocks, *cuts[j])

        total = None
        for j in range(len(cuts) - 1):
            while len(state["terms"]) <= j:
                yield ()
            state["terms"][j] = yield state["terms"][j]
            (total,) = yield add_products(total, [term(j)])
        while len(state["terms"]) < len(cuts) or "adapter_terms" not in state:
            yield ()
        total, state["terms"][-1] = yield (total, state["terms"][-1])
        late = [term(len(cuts) - 1)] + state["adapter_terms"]
        hidden_grad, gate_part = yield add_products(total, late, (gate, hidden))
        state["rows"] = (hidden_grad, lax.psum(gate_part[:, 0], "tp"))

    def adapters():
        parts = [adapter_down.T[None], adapter_up[None]]
        paths = [chip_bits, chip_bits[::-1]]
        for step in range(len(chip_bits)):
            got = yield [flip(part, bits[step]) for part, bits in zip(parts, paths)]
            parts = [jnp.concatenate(two, axis=0) for two in zip(parts, got)]
        splits = rank // rank_rows

        def wide(values, part):
            return lax.dot_general(
                values, part.reshape(-1, width), contract_last, preferred_element_type=f32
            )

        sources = (hidden, dy)
        got, first = yield (
            [flip(part, 0) for part in parts],
            [wide(values, part) for values, part in zip(sources, parts)],
        )
        blocks, products = [], []
        for values, part, other, product, bits in zip(sources, parts, got, first, paths):
            masks = masks_of(bits)
            blocks.append([(part, masks), (other, [m ^ 1 for m in masks])])
            products.append([(product, masks), (wide(values, other), [m ^ 1 for m in masks])])

        def select(products):
            out = [0.0] * splits
            for product, masks in products:
                for i, mask in enumerate(masks):
                    device = me ^ mask
                    here = depth == (device // splits + 1).astype(f32)
                    block = product[:, i * rank_rows : (i + 1) * rank_rows]
                    for h in range(splits):
                        out[h] += jnp.where((here & (device % splits == h))[:, None], block, 0.0)
            return out

        part = jnp.concatenate(select(products[0]) + select(products[1]), axis=1)
        part, blocks = yield (part, blocks[0])
        below = above = jnp.zeros_like(part)
        while state["step"] not in (0, min(2, planes - 1)):
            part = yield part
        for k in range(1, planes):
            sent = part + jnp.where(plane == k - 1, below, above)
            got = lax.ppermute(
                sent.astype(bf16), "tp", [(k - 1, k), (planes - k, planes - k - 1)]
            )
            if k == planes - 2 and state["step"]:
                state["hold"] = True
            got = yield got
            below = below + jnp.where(plane == k, got.astype(f32), 0.0)
            above = above + jnp.where(plane == planes - k - 1, got.astype(f32), 0.0)
        summed = part + below + above
        down, up = summed[:, :rank], adapter_scale * summed[:, rank:]

        def spread(masks):
            out = []
            for mask in masks:
                device = me ^ mask
                here = depth == (device // splits + 1).astype(f32)
                block = lax.dynamic_slice_in_dim(up, device % splits * rank_rows, rank_rows, axis=1)
                out.append(jnp.where(here[:, None], block, 0.0).astype(bf16))
            return jnp.concatenate(out, axis=1)

        state["adapter_terms"] = [
            (spread(masks), gathered, 0, rank_rows) for gathered, masks in blocks
        ]
        grads = jnp.concatenate(
            [gate[:, None] * up, gate[:, None] * adapter_scale * down], axis=1
        ).astype(bf16)
        grads, other_grads = yield (grads, flip(grads, 0))
        other_hidden, other_dy, other_depth = state["other"]

        def rank_columns(values, depths):
            parts = []
            for m in order:
                start = ((chip ^ m) * 2 + core) * rank_rows
                part = lax.dynamic_slice_in_dim(values, start % rank, rank_rows, axis=1)
                here = depths == (start // rank + 1).astype(f32)
                parts.append(jnp.where(here[:, None], part, jnp.zeros((), bf16)))
            return jnp.concatenate(parts, axis=1)

        jobs = []
        for at, own, other, bits in (
            (0, hidden, other_hidden, chip_bits),
            (rank, dy, other_dy, chip_bits[::-1]),
        ):
            pairs = [
                (rank_columns(grads[:, at : at + rank], depth), own),
                (rank_columns(other_grads[:, at : at + rank], other_depth), other),
            ]
            jobs.append((pairs, bits))
        state["adapter_grads"] = yield from scatter(jobs, rank_rows)

    count = range(len(cuts))
    run(
        [line(), weights(), adapters()]
        + [weight_chunk(j) for j in range(len(cuts))]
        + [rows_of_pre()]
    )
    hidden_grad, gate_grad = state["rows"]
    down_grad, up_grad = state["adapter_grads"]
    return (hidden_grad, gate_grad, state["weight"], down_grad, up_grad)


def solution(mesh):
    in_specs = (
        P("seq", "tp"),
        P("seq", "tp"),
        P("seq"),
        P("seq"),
        P(),
        P(None, "tp"),
        P("tp", "seq"),
        P("seq", "tp"),
    )
    out_specs = (P("seq", "tp"), P("seq"), P("seq", "tp"), P("seq", "tp"), P("seq", "tp"))
    return jax.shard_map(local, mesh=mesh, in_specs=in_specs, out_specs=out_specs, check_vma=False)
```

```python
import jax
import jax.numpy as jnp
from jax import lax
from jax.experimental import pallas as pl
from jax.experimental.pallas import tpu as pltpu
from jax.sharding import PartitionSpec as P

NREC = 4
LANES = 128
adapter_scale = 0.5
contract_rows = (((0,), (0,)), ((), ()))
contract_last = (((1,), (1,)), ((), ()))
f32 = jnp.float32
bf16 = jnp.bfloat16


def dot_rows(pairs):
    return sum(
        lax.dot_general(a, b, contract_rows, preferred_element_type=f32) for a, b in pairs
    )


def flip(value, bit):
    size = lax.axis_size("seq")
    return lax.ppermute(value, "seq", [(i, i ^ (1 << bit)) for i in range(size)])


def run(streams):
    results = [None] * len(streams)
    alive = dict(enumerate(streams))
    while alive:
        made = {}
        for i in list(alive):
            try:
                made[i] = alive[i].send(results[i])
            except StopIteration:
                del alive[i]
                results[i] = None
        held = lax.optimization_barrier(made)
        for i, values in held.items():
            results[i] = values


def chunk_sizes(units):
    first = -(-2 * units // 8)
    second = (units - first + 1) // 2
    return [size for size in (first, second, units - first - second) if size]


def add_products(total, terms, closing=None):
    rows, width = terms[0][0].shape[0], terms[0][1].shape[2]
    wide = min(width, 512)
    tiles = width // wide

    def kernel(*refs):
        refs = list(refs)
        done = refs.pop(0)[...] if total is not None else None
        for left, right, _, cut in terms:
            left_ref, right_ref = refs.pop(0), refs.pop(0)
            term = jnp.dot(
                left_ref[...],
                right_ref[...].reshape(right.shape[0] * cut, wide),
                preferred_element_type=f32,
            )
            done = term if done is None else done + term
        if closing is not None:
            scale_ref, hidden_ref, out_ref, sum_ref = refs
            part = jnp.sum(hidden_ref[...].astype(f32) * done, axis=1, keepdims=True)
            first = pl.program_id(0) == 0

            @pl.when(first)
            def _():
                sum_ref[...] = part

            @pl.when(jnp.logical_not(first))
            def _():
                sum_ref[...] += part

            done = scale_ref[...] * done
        else:
            (out_ref,) = refs
        out_ref[...] = done

    in_specs, operands = [], []
    tile = pl.BlockSpec((rows, wide), lambda n: (0, n))
    column = pl.BlockSpec((rows, 1), lambda n: (0, 0))
    if total is not None:
        operands.append(total)
        in_specs.append(tile)
    for left, right, start, cut in terms:
        groups = right.shape[0]
        operands += [left, right]
        in_specs += [
            pl.BlockSpec((rows, groups * cut), lambda n: (0, 0)),
            pl.BlockSpec(
                (pl.Element(groups), pl.Element(cut), pl.Element(wide)),
                lambda n, start=start: (0, start, n * wide),
            ),
        ]
    out_shape, out_specs = [jax.ShapeDtypeStruct((rows, width), f32)], [tile]
    if closing is not None:
        operands += [closing[0][:, None], closing[1]]
        in_specs += [column, tile]
        out_shape.append(jax.ShapeDtypeStruct((rows, 1), f32))
        out_specs.append(column)
    return pl.pallas_call(
        kernel,
        grid=(tiles,),
        in_specs=in_specs,
        out_specs=out_specs,
        out_shape=out_shape,
        input_output_aliases={0: 0} if total is not None else {},
        compiler_params=pltpu.CompilerParams(vmem_limit_bytes=48 * 2**20),
        cost_estimate=pl.CostEstimate(flops=0, bytes_accessed=0, transcendentals=0),
    )(*operands)


def masks_of(bits):
    masks = [0]
    for bit in bits:
        masks = masks + [m | (1 << bit) for m in masks]
    return masks


def column_products(lefts, rights, cut, picks, moving, added=None):
    depth, columns = lefts[0].shape
    half = rights[0].shape[1] // 2
    pairs = len(lefts)
    wide = min(half, 512)
    per = half // wide
    count = len(picks[0])
    kinds = [(moving, bf16)] * (moving > 0) + [(count - moving, f32)] * (count > moving)

    def kernel(*refs):
        left_refs, right_refs, refs = refs[:pairs], refs[pairs : 2 * pairs], refs[2 * pairs :]
        added_refs = refs[:2] if added is not None else None
        out_refs = refs[2 if added is not None else 0 :]
        for h in range(2):

            @pl.when(pl.program_id(0) // per == h)
            def _():
                chosen = [
                    jnp.concatenate(
                        [left_ref[:, p * cut : (p + 1) * cut] for p in picks[h]], axis=1
                    )
                    for left_ref in left_refs
                ]
                term = dot_rows([(a, ref[...]) for a, ref in zip(chosen, right_refs)])
                if added_refs is not None:
                    term = term + added_refs[h][...].astype(f32)
                first = 0
                for i, (blocks, kind) in enumerate(kinds):
                    out_refs[2 * i + h][...] = term[first : first + blocks * cut].astype(kind)
                    first += blocks * cut

    def halves(blocks):
        return [
            pl.BlockSpec((blocks * cut, wide), lambda n: (0, jnp.minimum(n, per - 1))),
            pl.BlockSpec((blocks * cut, wide), lambda n: (0, jnp.maximum(n - per, 0))),
        ]

    return pl.pallas_call(
        kernel,
        grid=(2 * per,),
        in_specs=[pl.BlockSpec((depth, columns), lambda n: (0, 0))] * pairs
        + [pl.BlockSpec((depth, wide), lambda n: (0, n))] * pairs
        + (halves(count) if added is not None else []),
        out_specs=[spec for blocks, _ in kinds for spec in halves(blocks)],
        out_shape=[
            jax.ShapeDtypeStruct((blocks * cut, half), kind)
            for blocks, kind in kinds
            for _ in range(2)
        ],
        compiler_params=pltpu.CompilerParams(vmem_limit_bytes=40 * 2**20),
        cost_estimate=pl.CostEstimate(flops=0, bytes_accessed=0, transcendentals=0),
    )(*lefts, *rights, *(added if added is not None else ()))


def lay_out(ups, downs, cut, order):
    planes, chips = lax.axis_size("tp"), len(order)
    rows, piece = ups[0].shape
    me = lax.axis_index("seq")
    where = jnp.stack([lax.axis_index("tp"), me >> 1, me & 1]).astype(jnp.int32)

    def kernel(where_ref, *refs):
        parts, (whole_ref, mine_ref, theirs_ref, whole, in_sem, out_sem) = refs[:-6], refs[-6:]
        plane, chip, core = where_ref[0], where_ref[1], where_ref[2]

        def place(part, b):
            return pltpu.make_async_copy(part, whole.at[:, b * piece : (b + 1) * piece], in_sem)

        for at, part in enumerate(parts):
            for b in range(planes):
                if 0 <= b - at + planes - 1 < planes:

                    @pl.when(plane == b - at + planes - 1)
                    def _():
                        place(part, b).start()

        for b in range(planes):
            place(parts[0], b).wait()
        copies = [pltpu.make_async_copy(whole, whole_ref, out_sem.at[0])]
        for at, mask in enumerate(order):
            for which, ref in ((core, mine_ref), (1 - core, theirs_ref)):
                column = pl.multiple_of(((chip ^ mask) * 2 + which) * cut, LANES)
                copies.append(
                    pltpu.make_async_copy(
                        whole.at[:, pl.ds(column, cut)],
                        ref.at[:, at * cut : (at + 1) * cut],
                        out_sem.at[len(copies)],
                    )
                )
        for copy in copies:
            copy.start()
        for copy in copies:
            copy.wait()

    parts = ups[:0:-1] + downs
    anywhere = pl.BlockSpec(memory_space=pl.ANY)
    return pl.pallas_call(
        kernel,
        in_specs=[pl.BlockSpec(memory_space=pltpu.SMEM)] + [anywhere] * len(parts),
        out_specs=[anywhere] * 3,
        out_shape=[
            jax.ShapeDtypeStruct((rows, planes * piece), bf16),
            jax.ShapeDtypeStruct((rows, chips * cut), bf16),
            jax.ShapeDtypeStruct((rows, chips * cut), bf16),
        ],
        scratch_shapes=[
            pltpu.VMEM((rows, planes * piece), bf16),
            pltpu.SemaphoreType.DMA,
            pltpu.SemaphoreType.DMA((1 + 2 * chips,)),
        ],
        compiler_params=pltpu.CompilerParams(vmem_limit_bytes=16 * 2**20),
        cost_estimate=pl.CostEstimate(flops=0, bytes_accessed=0, transcendentals=0),
    )(where, *parts)


def local(
    hidden,
    cotangent,
    router_gate,
    recursion_depth,
    live_counts,
    out_weight,
    adapter_down,
    adapter_up,
):
    shards, planes = lax.axis_size("seq"), lax.axis_size("tp")
    me, plane = lax.axis_index("seq"), lax.axis_index("tp")
    core, chip = me & 1, me >> 1
    chips = shards // 2
    chip_bits = list(range(1, shards.bit_length() - 1))
    rows, width = hidden.shape
    own_outs = width * planes // shards
    per_block = width // own_outs
    rank_rows = adapter_up.shape[0]
    rank = rank_rows * shards // NREC
    half = width // 2
    order = [i ^ (i >> 1) for i in range(chips)]
    cuts, first = [], 0
    for share in chunk_sizes(own_outs // LANES):
        cuts.append((first, share * LANES))
        first += share * LANES

    live = jnp.arange(rows, dtype=jnp.int32) < lax.dynamic_index_in_dim(live_counts, me, 0, False)
    live_gate = jnp.where(live, router_gate, jnp.zeros((), bf16))
    gate, depth = live_gate.astype(f32), recursion_depth.astype(f32)
    state = {"whole": {}, "step": 0, "weight": jnp.zeros((own_outs, width), f32)}

    pieces = [
        jnp.concatenate(
            [cotangent[:, i * own_outs + start : i * own_outs + start + cut] for i in range(per_block)],
            axis=1,
        )
        for start, cut in cuts
    ]

    def line():
        later = pieces
        for j in range(len(cuts)):
            ups, downs = [later[0]], [later[0]]
            later = later[1:]
            for k in range(1, planes):
                state["step"] = k
                up = lax.ppermute(ups[-1], "tp", [(i, i + 1) for i in range(k - 1, planes - 1)])
                down = lax.ppermute(downs[-1], "tp", [(i, i - 1) for i in range(1, planes - k + 1)])
                if k < planes - 1:
                    up, down, later = yield (up, down, later)
                else:
                    up, down = yield (up, down)
                ups.append(up)
                downs.append(down)
            state["whole"][j] = (ups, downs)
        state["step"] = 0

    def columns(values, size, wanted):
        spots = [order.index(m) for m in wanted]
        lo, hi = min(spots), max(spots)
        if hi - lo + 1 == len(spots):
            return values[:, lo * size : (hi + 1) * size], [order[i] for i in range(lo, hi + 1)]
        return jnp.concatenate([values[:, i * size : (i + 1) * size] for i in spots], axis=1), wanted

    def scatter(jobs, size):
        sums, sent = [], []
        for pairs, bits in jobs:
            first_bit = bits[0] - 1
            away = [m for m in range(chips) if m >> first_bit & 1]
            away_pairs = [(columns(a, size, away)[0], b) for a, b in pairs]
            sent.append((dot_rows(away_pairs).astype(bf16), columns(pairs[0][0], size, away)[1]))
            sums.append({})
        made = yield [values for values, _ in sent]
        made = yield [flip(values, bits[0]) for values, (_, bits) in zip(made, jobs)]
        for step in range(1, len(chip_bits) + 1):
            sent_before, sent = sent, []
            for total, got, (_, at), (pairs, bits) in zip(sums, made, sent_before, jobs):
                before = 1 << (bits[step - 1] - 1)
                arrived = {
                    m ^ before: got[i * size : (i + 1) * size].astype(f32) for i, m in enumerate(at)
                }
                for m in arrived:
                    own = total.pop(m, None)
                    if own is None:
                        own = dot_rows([(columns(a, size, [m])[0], b) for a, b in pairs])
                    total[m] = own + arrived[m]
                if step < len(chip_bits):
                    moving = [m for m in total if m >> (bits[step] - 1) & 1]
                    sent.append(([total.pop(m).astype(bf16) for m in moving], moving))
            if step < len(chip_bits):
                made = [jnp.concatenate(values, axis=0) for values, _ in sent]
                made = [flip(values, bits[step]) for values, (_, bits) in zip(made, jobs)]
                made, sums = yield (made, sums)
        return [total[0] for total in sums]

    def weights():
        small = jnp.stack([live_gate, recursion_depth.astype(bf16)])
        other_small, now = yield (flip(small, 0), hidden)
        other_hidden = flip(now, 0)
        gated = (gate[:, None] * hidden.astype(f32)).astype(bf16)
        other_hidden, gated, now, state["weight"] = yield (
            other_hidden, gated, cotangent, state["weight"]
        )
        other_dy = flip(now, 0)
        other_gate, other_depth = other_small[0].astype(f32), other_small[1].astype(f32)
        other_gated = (other_gate[:, None] * other_hidden.astype(f32)).astype(bf16)
        state["other"] = yield (other_hidden, other_dy, other_depth)
        state["gated"] = (gated, other_gated)

    def weight_chunk(j):
        start, cut = cuts[j]
        while j not in state["whole"]:
            yield ()
        whole, mine, theirs = lay_out(*state["whole"][j], cut, order)
        left = (mine, flip(theirs, 0))
        state["theirs"] = left[1]
        state["terms"].append(whole)
        paths = [[bit - 1 for bit in chip_bits], [bit - 1 for bit in chip_bits[::-1]]]
        stay = []
        for bits in paths:
            kept = [m for m in range(chips) if not m >> bits[0] & 1]
            if len(bits) > 1:
                gone = [m for m in kept if m >> bits[1] & 1]
                kept = gone + [m ^ 1 << bits[1] for m in gone]
            stay.append(kept)
        away = [[m | 1 << bits[0] for m in kept] for kept, bits in zip(stay, paths)]
        spots = [[order.index(m) for m in kept] for kept in away]
        sent = column_products(left, state["gated"], cut, spots, len(spots[0]))
        sent, left = yield (sent, left)
        got = [flip(values, bits[0] + 1) for values, bits in zip(sent, paths)]
        if j < len(cuts) - 1:
            yield ()
        got = yield got
        if state["step"] == 1:
            got = lax.optimization_barrier((got, state["theirs"]))[0]
        spots = [[order.index(m) for m in kept] for kept in stay]
        parts = column_products(left, state["gated"], cut, spots, chips // 4, got)
        moved, rest = (parts[:2], parts[2:]) if len(parts) > 2 else (None, parts)
        for step in range(1, len(chip_bits)):
            got, rest = yield ([flip(values, bits[step] + 1) for values, bits in zip(moved, paths)], rest)
            rest = [own + new.astype(f32) for own, new in zip(rest, got)]
            stay = [kept[len(kept) // 2 :] for kept in stay]
            if step + 1 < len(chip_bits):
                moved, after = [], []
                for total, kept, bits in zip(rest, stay, paths):
                    place = {m: total[i * cut : (i + 1) * cut] for i, m in enumerate(kept)}
                    gone = [m for m in kept if m >> bits[step + 1] & 1]
                    moved.append(jnp.concatenate([place[m].astype(bf16) for m in gone], axis=0))
                    after.append([place[m ^ 1 << bits[step + 1]] for m in gone])
                    kept[:] = gone + [m ^ 1 << bits[step + 1] for m in gone]
                rest = [jnp.concatenate(values, axis=0) for values in after]
        state["weight"] = lax.dynamic_update_slice(
            state["weight"], jnp.concatenate(rest, axis=1), (start, 0)
        )

    state["terms"] = []

    def rows_of_pre():
        weight_blocks = out_weight.reshape(shards, own_outs, width)

        def term(j):
            return (state["terms"][j], weight_blocks, *cuts[j])

        total = None
        for j in range(len(cuts) - 1):
            while len(state["terms"]) <= j:
                yield ()
            for _ in range(2):
                state["terms"][j] = yield state["terms"][j]
            (total,) = yield add_products(total, [term(j)])
        while len(state["terms"]) < len(cuts) or "adapter_terms" not in state:
            yield ()
        total, state["terms"][-1] = yield (total, state["terms"][-1])
        late = [term(len(cuts) - 1)] + state["adapter_terms"]
        hidden_grad, gate_part = yield add_products(total, late, (gate, hidden))
        gate_sum = jnp.where(live, gate_part[:, 0], 0.0)
        step = 1
        while step < planes:
            pairs = [(i, i ^ step) for i in range(planes)]
            gate_sum = gate_sum + lax.ppermute(gate_sum, "tp", pairs)
            step *= 2
        state["rows"] = (hidden_grad, gate_sum)

    def adapters():
        parts = [adapter_down.T[None], adapter_up[None]]
        paths = [chip_bits, chip_bits[::-1]]
        for step in range(len(chip_bits)):
            got = yield [flip(part, bits[step]) for part, bits in zip(parts, paths)]
            parts = [jnp.concatenate(two, axis=0) for two in zip(parts, got)]
        splits = rank // rank_rows

        def wide(values, part):
            return lax.dot_general(
                values, part.reshape(-1, width), contract_last, preferred_element_type=f32
            )

        sources = (hidden, cotangent)
        got = [flip(part, 0) for part in parts]
        first = [wide(values, part) for values, part in zip(sources, parts)]
        second = [wide(values, part) for values, part in zip(sources, got)]
        got, first, second = yield (got, first, second)
        blocks, products = [], []
        for i, bits in enumerate(paths):
            masks = masks_of(bits)
            others = [m ^ 1 for m in masks]
            blocks.append([(parts[i], masks), (got[i], others)])
            products.append([(first[i], masks), (second[i], others)])

        def select(products):
            out = [0.0] * splits
            for product, masks in products:
                for i, mask in enumerate(masks):
                    device = me ^ mask
                    here = depth == (device // splits + 1).astype(f32)
                    block = product[:, i * rank_rows : (i + 1) * rank_rows]
                    for h in range(splits):
                        out[h] += jnp.where((here & (device % splits == h))[:, None], block, 0.0)
            return out

        part = jnp.concatenate(select(products[0]) + select(products[1]), axis=1)
        part, blocks = yield (part, blocks[0])
        below = above = jnp.zeros_like(part)
        while state["step"] not in (0, min(2, planes - 1)):
            part = yield part
        for k in range(1, planes):
            sent = part + jnp.where(plane == k - 1, below, above)
            got = lax.ppermute(
                sent.astype(bf16), "tp", [(k - 1, k), (planes - k, planes - k - 1)]
            )
            got = yield got
            below = below + jnp.where(plane == k, got.astype(f32), 0.0)
            above = above + jnp.where(plane == planes - k - 1, got.astype(f32), 0.0)
        summed = part + below + above
        down, up = summed[:, :rank], adapter_scale * summed[:, rank:]

        def spread(masks):
            out = []
            for mask in masks:
                device = me ^ mask
                here = depth == (device // splits + 1).astype(f32)
                block = lax.dynamic_slice_in_dim(up, device % splits * rank_rows, rank_rows, axis=1)
                out.append(jnp.where(here[:, None], block, 0.0).astype(bf16))
            return jnp.concatenate(out, axis=1)

        state["adapter_terms"] = [
            (spread(masks), gathered, 0, rank_rows) for gathered, masks in blocks
        ]
        grads = jnp.concatenate(
            [gate[:, None] * up, gate[:, None] * adapter_scale * down], axis=1
        ).astype(bf16)
        other_grads = flip(grads, 0)
        other_hidden, other_dy, other_depth = state["other"]

        def rank_columns(values, depths):
            parts = []
            for m in order:
                start = ((chip ^ m) * 2 + core) * rank_rows
                part = lax.dynamic_slice_in_dim(values, start % rank, rank_rows, axis=1)
                here = depths == (start // rank + 1).astype(f32)
                parts.append(jnp.where(here[:, None], part, jnp.zeros((), bf16)))
            return jnp.concatenate(parts, axis=1)

        jobs = []
        for at, own, other, bits in (
            (0, hidden, other_hidden, chip_bits),
            (rank, cotangent, other_dy, chip_bits[::-1]),
        ):
            pairs = [
                (rank_columns(grads[:, at : at + rank], depth), own),
                (rank_columns(other_grads[:, at : at + rank], other_depth), other),
            ]
            jobs.append((pairs, bits))
        state["adapter_grads"] = yield from scatter(jobs, rank_rows)

    count = range(len(cuts))
    run(
        [line(), weights(), adapters()]
        + [weight_chunk(j) for j in reversed(range(len(cuts)))]
        + [rows_of_pre()]
    )
    hidden_grad, gate_grad = state["rows"]
    down_grad, up_grad = state["adapter_grads"]
    return (hidden_grad, gate_grad, state["weight"], down_grad, up_grad)


def solution(mesh):
    in_specs = (
        P("seq", "tp"),
        P("seq", "tp"),
        P("seq"),
        P("seq"),
        P(),
        P(None, "tp"),
        P("tp", "seq"),
        P("seq", "tp"),
    )
    out_specs = (P("seq", "tp"), P("seq"), P("seq", "tp"), P("seq", "tp"), P("seq", "tp"))
    return jax.shard_map(local, mesh=mesh, in_specs=in_specs, out_specs=out_specs, check_vma=False)
```

```python
import jax
import jax.numpy as jnp
from jax import lax
from jax.experimental import pallas as pl
from jax.experimental.pallas import tpu as pltpu
from jax.sharding import PartitionSpec as P

NREC = 4
LANES = 128
adapter_scale = 0.5
contract_rows = (((0,), (0,)), ((), ()))
contract_last = (((1,), (1,)), ((), ()))
f32 = jnp.float32
bf16 = jnp.bfloat16


def dot_rows(pairs):
    return sum(
        lax.dot_general(a, b, contract_rows, preferred_element_type=f32) for a, b in pairs
    )


def flip(value, bit):
    size = lax.axis_size("seq")
    return lax.ppermute(value, "seq", [(i, i ^ (1 << bit)) for i in range(size)])


def run(streams):
    results = [None] * len(streams)
    alive = dict(enumerate(streams))
    while alive:
        made = {}
        for i in list(alive):
            try:
                made[i] = alive[i].send(results[i])
            except StopIteration:
                del alive[i]
                results[i] = None
        held = lax.optimization_barrier(made)
        for i, values in held.items():
            results[i] = values


def chunk_sizes(units):
    first = -(-2 * units // 8)
    second = (units - first + 1) // 2
    return [size for size in (first, second, units - first - second) if size]


def add_products(total, terms, closing=None):
    rows, width = terms[0][0].shape[0], terms[0][1].shape[2]
    wide = min(width, 512)
    tiles = width // wide

    def kernel(*refs):
        refs = list(refs)
        done = refs.pop(0)[...] if total is not None else None
        for left, right, _, cut in terms:
            left_ref, right_ref = refs.pop(0), refs.pop(0)
            term = jnp.dot(
                left_ref[...],
                right_ref[...].reshape(right.shape[0] * cut, wide),
                preferred_element_type=f32,
            )
            done = term if done is None else done + term
        if closing is not None:
            scale_ref, hidden_ref, out_ref, sum_ref = refs
            part = jnp.sum(hidden_ref[...].astype(f32) * done, axis=1, keepdims=True)
            first = pl.program_id(0) == 0

            @pl.when(first)
            def _():
                sum_ref[...] = part

            @pl.when(jnp.logical_not(first))
            def _():
                sum_ref[...] += part

            done = scale_ref[...] * done
        else:
            (out_ref,) = refs
        out_ref[...] = done

    in_specs, operands = [], []
    tile = pl.BlockSpec((rows, wide), lambda n: (0, n))
    column = pl.BlockSpec((rows, 1), lambda n: (0, 0))
    if total is not None:
        operands.append(total)
        in_specs.append(tile)
    for left, right, start, cut in terms:
        groups = right.shape[0]
        operands += [left, right]
        in_specs += [
            pl.BlockSpec((rows, groups * cut), lambda n: (0, 0)),
            pl.BlockSpec(
                (pl.Element(groups), pl.Element(cut), pl.Element(wide)),
                lambda n, start=start: (0, start, n * wide),
            ),
        ]
    out_shape, out_specs = [jax.ShapeDtypeStruct((rows, width), f32)], [tile]
    if closing is not None:
        operands += [closing[0][:, None], closing[1]]
        in_specs += [column, tile]
        out_shape.append(jax.ShapeDtypeStruct((rows, 1), f32))
        out_specs.append(column)
    return pl.pallas_call(
        kernel,
        grid=(tiles,),
        in_specs=in_specs,
        out_specs=out_specs,
        out_shape=out_shape,
        input_output_aliases={0: 0} if total is not None else {},
        compiler_params=pltpu.CompilerParams(vmem_limit_bytes=48 * 2**20),
        cost_estimate=pl.CostEstimate(flops=0, bytes_accessed=0, transcendentals=0),
    )(*operands)


def masks_of(bits):
    masks = [0]
    for bit in bits:
        masks = masks + [m | (1 << bit) for m in masks]
    return masks


def column_products(lefts, rights, cut, picks, moving, added=None):
    depth, columns = lefts[0].shape
    half = rights[0].shape[1] // 2
    pairs = len(lefts)
    wide = min(half, 512)
    per = half // wide
    count = len(picks[0])
    kinds = [(moving, bf16)] * (moving > 0) + [(count - moving, f32)] * (count > moving)

    def kernel(*refs):
        left_refs, right_refs, refs = refs[:pairs], refs[pairs : 2 * pairs], refs[2 * pairs :]
        added_refs = refs[:2] if added is not None else None
        out_refs = refs[2 if added is not None else 0 :]
        for h in range(2):

            @pl.when(pl.program_id(0) // per == h)
            def _():
                chosen = [
                    jnp.concatenate(
                        [left_ref[:, p * cut : (p + 1) * cut] for p in picks[h]], axis=1
                    )
                    for left_ref in left_refs
                ]
                term = dot_rows([(a, ref[...]) for a, ref in zip(chosen, right_refs)])
                if added_refs is not None:
                    term = term + added_refs[h][...].astype(f32)
                first = 0
                for i, (blocks, kind) in enumerate(kinds):
                    out_refs[2 * i + h][...] = term[first : first + blocks * cut].astype(kind)
                    first += blocks * cut

    def halves(blocks):
        return [
            pl.BlockSpec((blocks * cut, wide), lambda n: (0, jnp.minimum(n, per - 1))),
            pl.BlockSpec((blocks * cut, wide), lambda n: (0, jnp.maximum(n - per, 0))),
        ]

    return pl.pallas_call(
        kernel,
        grid=(2 * per,),
        in_specs=[pl.BlockSpec((depth, columns), lambda n: (0, 0))] * pairs
        + [pl.BlockSpec((depth, wide), lambda n: (0, n))] * pairs
        + (halves(count) if added is not None else []),
        out_specs=[spec for blocks, _ in kinds for spec in halves(blocks)],
        out_shape=[
            jax.ShapeDtypeStruct((blocks * cut, half), kind)
            for blocks, kind in kinds
            for _ in range(2)
        ],
        compiler_params=pltpu.CompilerParams(vmem_limit_bytes=40 * 2**20),
        cost_estimate=pl.CostEstimate(flops=0, bytes_accessed=0, transcendentals=0),
    )(*lefts, *rights, *(added if added is not None else ()))


def lay_out(ups, downs, cut, order):
    planes, chips = lax.axis_size("tp"), len(order)
    rows, piece = ups[0].shape
    me = lax.axis_index("seq")
    where = jnp.stack([lax.axis_index("tp"), me >> 1, me & 1]).astype(jnp.int32)

    def kernel(where_ref, *refs):
        parts, (whole_ref, mine_ref, theirs_ref, whole, in_sem, out_sem) = refs[:-6], refs[-6:]
        plane, chip, core = where_ref[0], where_ref[1], where_ref[2]

        def place(part, b):
            return pltpu.make_async_copy(part, whole.at[:, b * piece : (b + 1) * piece], in_sem)

        for at, part in enumerate(parts):
            for b in range(planes):
                if 0 <= b - at + planes - 1 < planes:

                    @pl.when(plane == b - at + planes - 1)
                    def _():
                        place(part, b).start()

        for b in range(planes):
            place(parts[0], b).wait()
        copies = [pltpu.make_async_copy(whole, whole_ref, out_sem.at[0])]
        for at, mask in enumerate(order):
            for which, ref in ((core, mine_ref), (1 - core, theirs_ref)):
                column = pl.multiple_of(((chip ^ mask) * 2 + which) * cut, LANES)
                copies.append(
                    pltpu.make_async_copy(
                        whole.at[:, pl.ds(column, cut)],
                        ref.at[:, at * cut : (at + 1) * cut],
                        out_sem.at[len(copies)],
                    )
                )
        for copy in copies:
            copy.start()
        for copy in copies:
            copy.wait()

    parts = ups[:0:-1] + downs
    anywhere = pl.BlockSpec(memory_space=pl.ANY)
    return pl.pallas_call(
        kernel,
        in_specs=[pl.BlockSpec(memory_space=pltpu.SMEM)] + [anywhere] * len(parts),
        out_specs=[anywhere] * 3,
        out_shape=[
            jax.ShapeDtypeStruct((rows, planes * piece), bf16),
            jax.ShapeDtypeStruct((rows, chips * cut), bf16),
            jax.ShapeDtypeStruct((rows, chips * cut), bf16),
        ],
        scratch_shapes=[
            pltpu.VMEM((rows, planes * piece), bf16),
            pltpu.SemaphoreType.DMA,
            pltpu.SemaphoreType.DMA((1 + 2 * chips,)),
        ],
        compiler_params=pltpu.CompilerParams(vmem_limit_bytes=16 * 2**20),
        cost_estimate=pl.CostEstimate(flops=0, bytes_accessed=0, transcendentals=0),
    )(where, *parts)


def local(
    hidden,
    cotangent,
    router_gate,
    recursion_depth,
    live_counts,
    out_weight,
    adapter_down,
    adapter_up,
):
    shards, planes = lax.axis_size("seq"), lax.axis_size("tp")
    me, plane = lax.axis_index("seq"), lax.axis_index("tp")
    core, chip = me & 1, me >> 1
    chips = shards // 2
    chip_bits = list(range(1, shards.bit_length() - 1))
    rows, width = hidden.shape
    own_outs = width * planes // shards
    per_block = width // own_outs
    rank_rows = adapter_up.shape[0]
    rank = rank_rows * shards // NREC
    half = width // 2
    order = [i ^ (i >> 1) for i in range(chips)]
    cuts, first = [], 0
    for share in chunk_sizes(own_outs // LANES):
        cuts.append((first, share * LANES))
        first += share * LANES

    live = jnp.arange(rows, dtype=jnp.int32) < lax.dynamic_index_in_dim(live_counts, me, 0, False)
    live_gate = jnp.where(live, router_gate, jnp.zeros((), bf16))
    gate, depth = live_gate.astype(f32), recursion_depth.astype(f32)
    state = {"whole": {}, "step": 0, "hold": False, "weight": jnp.zeros((own_outs, width), f32)}

    pieces = [
        jnp.concatenate(
            [cotangent[:, i * own_outs + start : i * own_outs + start + cut] for i in range(per_block)],
            axis=1,
        )
        for start, cut in cuts
    ]

    def line():
        later = pieces
        for j in range(len(cuts)):
            ups, downs = [later[0]], [later[0]]
            for k in range(1, planes):
                if state["hold"]:
                    state["hold"], state["step"] = False, -1
                    yield ()
                state["step"] = k
                up = lax.ppermute(ups[-1], "tp", [(i, i + 1) for i in range(k - 1, planes - 1)])
                down = lax.ppermute(downs[-1], "tp", [(i, i - 1) for i in range(1, planes - k + 1)])
                if k == 1:
                    later = later[1:]
                if k < planes - 1:
                    up, down, later = yield (up, down, later)
                else:
                    up, down = yield (up, down)
                ups.append(up)
                downs.append(down)
            state["whole"][j] = (ups, downs)
        state["step"] = 0

    def columns(values, size, wanted):
        spots = [order.index(m) for m in wanted]
        lo, hi = min(spots), max(spots)
        if hi - lo + 1 == len(spots):
            return values[:, lo * size : (hi + 1) * size], [order[i] for i in range(lo, hi + 1)]
        return jnp.concatenate([values[:, i * size : (i + 1) * size] for i in spots], axis=1), wanted

    def scatter(jobs, size):
        sums, sent = [], []
        for pairs, bits in jobs:
            first_bit = bits[0] - 1
            away = [m for m in range(chips) if m >> first_bit & 1]
            away_pairs = [(columns(a, size, away)[0], b) for a, b in pairs]
            sent.append((dot_rows(away_pairs).astype(bf16), columns(pairs[0][0], size, away)[1]))
            sums.append({})
        made = yield [values for values, _ in sent]
        while state["step"] not in (0, planes - 1):
            made = yield made
        made = yield [flip(values, bits[0]) for values, (_, bits) in zip(made, jobs)]
        for step in range(1, len(chip_bits) + 1):
            sent_before, sent = sent, []
            for total, got, (_, at), (pairs, bits) in zip(sums, made, sent_before, jobs):
                before = 1 << (bits[step - 1] - 1)
                arrived = {
                    m ^ before: got[i * size : (i + 1) * size].astype(f32) for i, m in enumerate(at)
                }
                for m in arrived:
                    own = total.pop(m, None)
                    if own is None:
                        own = dot_rows([(columns(a, size, [m])[0], b) for a, b in pairs])
                    total[m] = own + arrived[m]
                if step < len(chip_bits):
                    moving = [m for m in total if m >> (bits[step] - 1) & 1]
                    sent.append(([total.pop(m).astype(bf16) for m in moving], moving))
            if step < len(chip_bits):
                made = [jnp.concatenate(values, axis=0) for values, _ in sent]
                made = [flip(values, bits[step]) for values, (_, bits) in zip(made, jobs)]
                made, sums = yield (made, sums)
        return [total[0] for total in sums]

    def weights():
        small = jnp.stack([live_gate, recursion_depth.astype(bf16)])
        other_small, now = yield (flip(small, 0), hidden)
        other_hidden = flip(now, 0)
        gated = (gate[:, None] * hidden.astype(f32)).astype(bf16)
        other_hidden, gated, now, state["weight"] = yield (
            other_hidden, gated, cotangent, state["weight"]
        )
        other_dy = flip(now, 0)
        other_gate, other_depth = other_small[0].astype(f32), other_small[1].astype(f32)
        other_gated = (other_gate[:, None] * other_hidden.astype(f32)).astype(bf16)
        state["other"] = yield (other_hidden, other_dy, other_depth)
        state["gated"] = (gated, other_gated)

    def weight_chunk(j):
        start, cut = cuts[j]
        while j not in state["whole"]:
            yield ()
        whole, mine, theirs = lay_out(*state["whole"][j], cut, order)
        left = (mine, flip(theirs, 0))
        state["theirs"] = left[1]
        state["terms"].append(whole)
        paths = [[bit - 1 for bit in chip_bits], [bit - 1 for bit in chip_bits[::-1]]]
        stay = []
        for bits in paths:
            kept = [m for m in range(chips) if not m >> bits[0] & 1]
            if len(bits) > 1:
                gone = [m for m in kept if m >> bits[1] & 1]
                kept = gone + [m ^ 1 << bits[1] for m in gone]
            stay.append(kept)
        away = [[m | 1 << bits[0] for m in kept] for kept, bits in zip(stay, paths)]
        spots = [[order.index(m) for m in kept] for kept in away]
        sent = column_products(left, state["gated"], cut, spots, len(spots[0]))
        sent, left = yield (sent, left)
        got = [flip(values, bits[0] + 1) for values, bits in zip(sent, paths)]
        got = yield got
        if state["step"] == 1:
            got = lax.optimization_barrier((got, state["theirs"]))[0]
        spots = [[order.index(m) for m in kept] for kept in stay]
        parts = column_products(left, state["gated"], cut, spots, chips // 4, got)
        moved, rest = (parts[:2], parts[2:]) if len(parts) > 2 else (None, parts)
        for step in range(1, len(chip_bits)):
            got, rest = yield ([flip(values, bits[step] + 1) for values, bits in zip(moved, paths)], rest)
            rest = [own + new.astype(f32) for own, new in zip(rest, got)]
            stay = [kept[len(kept) // 2 :] for kept in stay]
            if step + 1 < len(chip_bits):
                moved, after = [], []
                for total, kept, bits in zip(rest, stay, paths):
                    place = {m: total[i * cut : (i + 1) * cut] for i, m in enumerate(kept)}
                    gone = [m for m in kept if m >> bits[step + 1] & 1]
                    moved.append(jnp.concatenate([place[m].astype(bf16) for m in gone], axis=0))
                    after.append([place[m ^ 1 << bits[step + 1]] for m in gone])
                    kept[:] = gone + [m ^ 1 << bits[step + 1] for m in gone]
                rest = [jnp.concatenate(values, axis=0) for values in after]
        state["weight"] = lax.dynamic_update_slice(
            state["weight"], jnp.concatenate(rest, axis=1), (start, 0)
        )

    state["terms"] = []

    def rows_of_pre():
        weight_blocks = out_weight.reshape(shards, own_outs, width)

        def term(j):
            return (state["terms"][j], weight_blocks, *cuts[j])

        total = None
        for j in range(len(cuts) - 1):
            while len(state["terms"]) <= j:
                yield ()
            for _ in range(2 if j == 0 else 3):
                state["terms"][j] = yield state["terms"][j]
            (total,) = yield add_products(total, [term(j)])
        while len(state["terms"]) < len(cuts) or "adapter_terms" not in state:
            yield ()
        total, state["terms"][-1] = yield (total, state["terms"][-1])
        late = [term(len(cuts) - 1)] + state["adapter_terms"]
        hidden_grad, gate_part = yield add_products(total, late, (gate, hidden))
        gate_sum = jnp.where(live, gate_part[:, 0], 0.0)
        step = 1
        while step < planes:
            pairs = [(i, i ^ step) for i in range(planes)]
            gate_sum = gate_sum + lax.ppermute(gate_sum, "tp", pairs)
            step *= 2
        state["rows"] = (hidden_grad, gate_sum)

    def adapters():
        parts = [adapter_down.T[None], adapter_up[None]]
        paths = [chip_bits, chip_bits[::-1]]
        for step in range(len(chip_bits)):
            got = yield [flip(part, bits[step]) for part, bits in zip(parts, paths)]
            parts = [jnp.concatenate(two, axis=0) for two in zip(parts, got)]
        splits = rank // rank_rows

        def wide(values, part):
            return lax.dot_general(
                values, part.reshape(-1, width), contract_last, preferred_element_type=f32
            )

        sources = (hidden, cotangent)
        got = [flip(part, 0) for part in parts]
        first = [wide(values, part) for values, part in zip(sources, parts)]
        second = [wide(values, part) for values, part in zip(sources, got)]
        got, first, second = yield (got, first, second)
        blocks, products = [], []
        for i, bits in enumerate(paths):
            masks = masks_of(bits)
            others = [m ^ 1 for m in masks]
            blocks.append([(parts[i], masks), (got[i], others)])
            products.append([(first[i], masks), (second[i], others)])

        def select(products):
            out = [0.0] * splits
            for product, masks in products:
                for i, mask in enumerate(masks):
                    device = me ^ mask
                    here = depth == (device // splits + 1).astype(f32)
                    block = product[:, i * rank_rows : (i + 1) * rank_rows]
                    for h in range(splits):
                        out[h] += jnp.where((here & (device % splits == h))[:, None], block, 0.0)
            return out

        part = jnp.concatenate(select(products[0]) + select(products[1]), axis=1)
        part, blocks = yield (part, blocks[0])
        below = above = jnp.zeros_like(part)
        while state["step"] not in (0, min(2, planes - 1)):
            part = yield part
        for k in range(1, planes):
            sent = part + jnp.where(plane == k - 1, below, above)
            got = lax.ppermute(
                sent.astype(bf16), "tp", [(k - 1, k), (planes - k, planes - k - 1)]
            )
            if k == planes - 2 and state["step"]:
                state["hold"] = True
            got = yield got
            below = below + jnp.where(plane == k, got.astype(f32), 0.0)
            above = above + jnp.where(plane == planes - k - 1, got.astype(f32), 0.0)
        summed = part + below + above
        down, up = summed[:, :rank], adapter_scale * summed[:, rank:]

        def spread(masks):
            out = []
            for mask in masks:
                device = me ^ mask
                here = depth == (device // splits + 1).astype(f32)
                block = lax.dynamic_slice_in_dim(up, device % splits * rank_rows, rank_rows, axis=1)
                out.append(jnp.where(here[:, None], block, 0.0).astype(bf16))
            return jnp.concatenate(out, axis=1)

        state["adapter_terms"] = [
            (spread(masks), gathered, 0, rank_rows) for gathered, masks in blocks
        ]
        grads = jnp.concatenate(
            [gate[:, None] * up, gate[:, None] * adapter_scale * down], axis=1
        ).astype(bf16)
        other_grads = flip(grads, 0)
        other_hidden, other_dy, other_depth = state["other"]

        def rank_columns(values, depths):
            parts = []
            for m in order:
                start = ((chip ^ m) * 2 + core) * rank_rows
                part = lax.dynamic_slice_in_dim(values, start % rank, rank_rows, axis=1)
                here = depths == (start // rank + 1).astype(f32)
                parts.append(jnp.where(here[:, None], part, jnp.zeros((), bf16)))
            return jnp.concatenate(parts, axis=1)

        jobs = []
        for at, own, other, bits in (
            (0, hidden, other_hidden, chip_bits),
            (rank, cotangent, other_dy, chip_bits[::-1]),
        ):
            pairs = [
                (rank_columns(grads[:, at : at + rank], depth), own),
                (rank_columns(other_grads[:, at : at + rank], other_depth), other),
            ]
            jobs.append((pairs, bits))
        state["adapter_grads"] = yield from scatter(jobs, rank_rows)

    count = range(len(cuts))
    run(
        [line(), weights(), adapters()]
        + [weight_chunk(j) for j in reversed(range(len(cuts)))]
        + [rows_of_pre()]
    )
    hidden_grad, gate_grad = state["rows"]
    down_grad, up_grad = state["adapter_grads"]
    return (hidden_grad, gate_grad, state["weight"], down_grad, up_grad)


def solution(mesh):
    in_specs = (
        P("seq", "tp"),
        P("seq", "tp"),
        P("seq"),
        P("seq"),
        P(),
        P(None, "tp"),
        P("tp", "seq"),
        P("seq", "tp"),
    )
    out_specs = (P("seq", "tp"), P("seq"), P("seq", "tp"), P("seq", "tp"), P("seq", "tp"))
    return jax.shard_map(local, mesh=mesh, in_specs=in_specs, out_specs=out_specs, check_vma=False)
```

```python
import jax
import jax.numpy as jnp
from jax import lax
from jax.experimental import pallas as pl
from jax.experimental.pallas import tpu as pltpu
from jax.sharding import PartitionSpec as P

NREC = 4
LANES = 128
adapter_scale = 0.5
contract_rows = (((0,), (0,)), ((), ()))
contract_last = (((1,), (1,)), ((), ()))
f32 = jnp.float32
bf16 = jnp.bfloat16


def dot_rows(pairs):
    return sum(
        lax.dot_general(a, b, contract_rows, preferred_element_type=f32) for a, b in pairs
    )


def flip(value, bit):
    size = lax.axis_size("seq")
    return lax.ppermute(value, "seq", [(i, i ^ (1 << bit)) for i in range(size)])


def run(streams):
    results = [None] * len(streams)
    alive = dict(enumerate(streams))
    while alive:
        made = {}
        for i in list(alive):
            try:
                made[i] = alive[i].send(results[i])
            except StopIteration:
                del alive[i]
                results[i] = None
        held = lax.optimization_barrier(made)
        for i, values in held.items():
            results[i] = values


def chunk_sizes(units):
    first = -(-2 * units // 8)
    second = (units - first + 1) // 2
    return [size for size in (first, second, units - first - second) if size]


def add_products(total, terms, closing=None):
    rows, width = terms[0][0].shape[0], terms[0][1].shape[2]
    wide = min(width, 512)
    tiles = width // wide

    def kernel(*refs):
        refs = list(refs)
        done = refs.pop(0)[...] if total is not None else None
        for left, right, _, cut in terms:
            left_ref, right_ref = refs.pop(0), refs.pop(0)
            term = jnp.dot(
                left_ref[...],
                right_ref[...].reshape(right.shape[0] * cut, wide),
                preferred_element_type=f32,
            )
            done = term if done is None else done + term
        if closing is not None:
            scale_ref, hidden_ref, out_ref, sum_ref = refs
            part = jnp.sum(hidden_ref[...].astype(f32) * done, axis=1, keepdims=True)
            first = pl.program_id(0) == 0

            @pl.when(first)
            def _():
                sum_ref[...] = part

            @pl.when(jnp.logical_not(first))
            def _():
                sum_ref[...] += part

            done = scale_ref[...] * done
        else:
            (out_ref,) = refs
        out_ref[...] = done

    in_specs, operands = [], []
    tile = pl.BlockSpec((rows, wide), lambda n: (0, n))
    column = pl.BlockSpec((rows, 1), lambda n: (0, 0))
    if total is not None:
        operands.append(total)
        in_specs.append(tile)
    for left, right, start, cut in terms:
        groups = right.shape[0]
        operands += [left, right]
        in_specs += [
            pl.BlockSpec((rows, groups * cut), lambda n: (0, 0)),
            pl.BlockSpec(
                (pl.Element(groups), pl.Element(cut), pl.Element(wide)),
                lambda n, start=start: (0, start, n * wide),
            ),
        ]
    out_shape, out_specs = [jax.ShapeDtypeStruct((rows, width), f32)], [tile]
    if closing is not None:
        operands += [closing[0][:, None], closing[1]]
        in_specs += [column, tile]
        out_shape.append(jax.ShapeDtypeStruct((rows, 1), f32))
        out_specs.append(column)
    return pl.pallas_call(
        kernel,
        grid=(tiles,),
        in_specs=in_specs,
        out_specs=out_specs,
        out_shape=out_shape,
        input_output_aliases={0: 0} if total is not None else {},
        compiler_params=pltpu.CompilerParams(vmem_limit_bytes=48 * 2**20),
        cost_estimate=pl.CostEstimate(flops=0, bytes_accessed=0, transcendentals=0),
    )(*operands)


def masks_of(bits):
    masks = [0]
    for bit in bits:
        masks = masks + [m | (1 << bit) for m in masks]
    return masks


def column_products(lefts, rights, cut, picks, moving, added=None):
    depth, columns = lefts[0].shape
    half = rights[0].shape[1] // 2
    pairs = len(lefts)
    wide = min(half, 512)
    per = half // wide
    count = len(picks[0])
    kinds = [(moving, bf16)] * (moving > 0) + [(count - moving, f32)] * (count > moving)

    def kernel(*refs):
        left_refs, right_refs, refs = refs[:pairs], refs[pairs : 2 * pairs], refs[2 * pairs :]
        added_refs = refs[:2] if added is not None else None
        out_refs = refs[2 if added is not None else 0 :]
        for h in range(2):

            @pl.when(pl.program_id(0) // per == h)
            def _():
                chosen = [
                    jnp.concatenate(
                        [left_ref[:, p * cut : (p + 1) * cut] for p in picks[h]], axis=1
                    )
                    for left_ref in left_refs
                ]
                term = dot_rows([(a, ref[...]) for a, ref in zip(chosen, right_refs)])
                if added_refs is not None:
                    term = term + added_refs[h][...].astype(f32)
                first = 0
                for i, (blocks, kind) in enumerate(kinds):
                    out_refs[2 * i + h][...] = term[first : first + blocks * cut].astype(kind)
                    first += blocks * cut

    def halves(blocks):
        return [
            pl.BlockSpec((blocks * cut, wide), lambda n: (0, jnp.minimum(n, per - 1))),
            pl.BlockSpec((blocks * cut, wide), lambda n: (0, jnp.maximum(n - per, 0))),
        ]

    return pl.pallas_call(
        kernel,
        grid=(2 * per,),
        in_specs=[pl.BlockSpec((depth, columns), lambda n: (0, 0))] * pairs
        + [pl.BlockSpec((depth, wide), lambda n: (0, n))] * pairs
        + (halves(count) if added is not None else []),
        out_specs=[spec for blocks, _ in kinds for spec in halves(blocks)],
        out_shape=[
            jax.ShapeDtypeStruct((blocks * cut, half), kind)
            for blocks, kind in kinds
            for _ in range(2)
        ],
        compiler_params=pltpu.CompilerParams(vmem_limit_bytes=40 * 2**20),
        cost_estimate=pl.CostEstimate(flops=0, bytes_accessed=0, transcendentals=0),
    )(*lefts, *rights, *(added if added is not None else ()))


def lay_out(ups, downs, cut, order):
    planes, chips = lax.axis_size("tp"), len(order)
    rows, piece = ups[0].shape
    me = lax.axis_index("seq")
    where = jnp.stack([lax.axis_index("tp"), me >> 1, me & 1]).astype(jnp.int32)

    def kernel(where_ref, *refs):
        parts, (whole_ref, mine_ref, theirs_ref, whole, in_sem, out_sem) = refs[:-6], refs[-6:]
        plane, chip, core = where_ref[0], where_ref[1], where_ref[2]

        def place(part, b):
            return pltpu.make_async_copy(part, whole.at[:, b * piece : (b + 1) * piece], in_sem)

        for at, part in enumerate(parts):
            for b in range(planes):
                if 0 <= b - at + planes - 1 < planes:

                    @pl.when(plane == b - at + planes - 1)
                    def _():
                        place(part, b).start()

        for b in range(planes):
            place(parts[0], b).wait()
        copies = [pltpu.make_async_copy(whole, whole_ref, out_sem.at[0])]
        for at, mask in enumerate(order):
            for which, ref in ((core, mine_ref), (1 - core, theirs_ref)):
                column = pl.multiple_of(((chip ^ mask) * 2 + which) * cut, LANES)
                copies.append(
                    pltpu.make_async_copy(
                        whole.at[:, pl.ds(column, cut)],
                        ref.at[:, at * cut : (at + 1) * cut],
                        out_sem.at[len(copies)],
                    )
                )
        for copy in copies:
            copy.start()
        for copy in copies:
            copy.wait()

    parts = ups[:0:-1] + downs
    anywhere = pl.BlockSpec(memory_space=pl.ANY)
    return pl.pallas_call(
        kernel,
        in_specs=[pl.BlockSpec(memory_space=pltpu.SMEM)] + [anywhere] * len(parts),
        out_specs=[anywhere] * 3,
        out_shape=[
            jax.ShapeDtypeStruct((rows, planes * piece), bf16),
            jax.ShapeDtypeStruct((rows, chips * cut), bf16),
            jax.ShapeDtypeStruct((rows, chips * cut), bf16),
        ],
        scratch_shapes=[
            pltpu.VMEM((rows, planes * piece), bf16),
            pltpu.SemaphoreType.DMA,
            pltpu.SemaphoreType.DMA((1 + 2 * chips,)),
        ],
        compiler_params=pltpu.CompilerParams(vmem_limit_bytes=16 * 2**20),
        cost_estimate=pl.CostEstimate(flops=0, bytes_accessed=0, transcendentals=0),
    )(where, *parts)


def local(
    hidden,
    cotangent,
    router_gate,
    recursion_depth,
    live_counts,
    out_weight,
    adapter_down,
    adapter_up,
):
    shards, planes = lax.axis_size("seq"), lax.axis_size("tp")
    me, plane = lax.axis_index("seq"), lax.axis_index("tp")
    core, chip = me & 1, me >> 1
    chips = shards // 2
    chip_bits = list(range(1, shards.bit_length() - 1))
    rows, width = hidden.shape
    own_outs = width * planes // shards
    per_block = width // own_outs
    rank_rows = adapter_up.shape[0]
    rank = rank_rows * shards // NREC
    half = width // 2
    order = [i ^ (i >> 1) for i in range(chips)]
    cuts, first = [], 0
    for share in chunk_sizes(own_outs // LANES):
        cuts.append((first, share * LANES))
        first += share * LANES

    live = jnp.arange(rows, dtype=jnp.int32) < lax.dynamic_index_in_dim(live_counts, me, 0, False)
    live_gate = jnp.where(live, router_gate, jnp.zeros((), bf16))
    gate, depth = live_gate.astype(f32), recursion_depth.astype(f32)
    state = {"whole": {}, "step": 0, "hold": False, "weight": jnp.zeros((own_outs, width), f32)}

    pieces = [
        jnp.concatenate(
            [cotangent[:, i * own_outs + start : i * own_outs + start + cut] for i in range(per_block)],
            axis=1,
        )
        for start, cut in cuts
    ]

    def line():
        later = pieces
        for j in range(len(cuts)):
            ups, downs = [later[0]], [later[0]]
            for k in range(1, planes):
                if state["hold"]:
                    state["hold"], state["step"] = False, -1
                    yield ()
                state["step"] = k
                up = lax.ppermute(ups[-1], "tp", [(i, i + 1) for i in range(k - 1, planes - 1)])
                down = lax.ppermute(downs[-1], "tp", [(i, i - 1) for i in range(1, planes - k + 1)])
                if k == 1:
                    later = later[1:]
                if k < planes - 1:
                    up, down, later = yield (up, down, later)
                else:
                    up, down = yield (up, down)
                ups.append(up)
                downs.append(down)
            state["whole"][j] = (ups, downs)
        state["step"] = 0

    def columns(values, size, wanted):
        spots = [order.index(m) for m in wanted]
        lo, hi = min(spots), max(spots)
        if hi - lo + 1 == len(spots):
            return values[:, lo * size : (hi + 1) * size], [order[i] for i in range(lo, hi + 1)]
        return jnp.concatenate([values[:, i * size : (i + 1) * size] for i in spots], axis=1), wanted

    def scatter(jobs, size):
        sums, sent = [], []
        for pairs, bits in jobs:
            first_bit = bits[0] - 1
            away = [m for m in range(chips) if m >> first_bit & 1]
            away_pairs = [(columns(a, size, away)[0], b) for a, b in pairs]
            sent.append((dot_rows(away_pairs).astype(bf16), columns(pairs[0][0], size, away)[1]))
            sums.append({})
        made = yield [values for values, _ in sent]
        while state["step"] not in (0, planes - 1):
            made = yield made
        made = yield [flip(values, bits[0]) for values, (_, bits) in zip(made, jobs)]
        for step in range(1, len(chip_bits) + 1):
            sent_before, sent = sent, []
            for total, got, (_, at), (pairs, bits) in zip(sums, made, sent_before, jobs):
                before = 1 << (bits[step - 1] - 1)
                arrived = {
                    m ^ before: got[i * size : (i + 1) * size].astype(f32) for i, m in enumerate(at)
                }
                for m in arrived:
                    own = total.pop(m, None)
                    if own is None:
                        own = dot_rows([(columns(a, size, [m])[0], b) for a, b in pairs])
                    total[m] = own + arrived[m]
                if step < len(chip_bits):
                    moving = [m for m in total if m >> (bits[step] - 1) & 1]
                    sent.append(([total.pop(m).astype(bf16) for m in moving], moving))
            if step < len(chip_bits):
                made = [jnp.concatenate(values, axis=0) for values, _ in sent]
                made = [flip(values, bits[step]) for values, (_, bits) in zip(made, jobs)]
                made, sums = yield (made, sums)
        return [total[0] for total in sums]

    def weights():
        small = jnp.stack([live_gate, recursion_depth.astype(bf16)])
        other_small, now = yield (flip(small, 0), hidden)
        other_hidden = flip(now, 0)
        gated = (gate[:, None] * hidden.astype(f32)).astype(bf16)
        other_hidden, gated, now, state["weight"] = yield (
            other_hidden, gated, cotangent, state["weight"]
        )
        other_dy = flip(now, 0)
        other_gate, other_depth = other_small[0].astype(f32), other_small[1].astype(f32)
        other_gated = (other_gate[:, None] * other_hidden.astype(f32)).astype(bf16)
        state["other"] = yield (other_hidden, other_dy, other_depth)
        state["gated"] = (gated, other_gated)

    def weight_chunk(j):
        start, cut = cuts[j]
        while j not in state["whole"]:
            yield ()
        whole, mine, theirs = lay_out(*state["whole"][j], cut, order)
        left = (mine, flip(theirs, 0))
        state["theirs"] = left[1]
        state["terms"].append(whole)
        paths = [[bit - 1 for bit in chip_bits], [bit - 1 for bit in chip_bits[::-1]]]
        stay = []
        for bits in paths:
            kept = [m for m in range(chips) if not m >> bits[0] & 1]
            if len(bits) > 1:
                gone = [m for m in kept if m >> bits[1] & 1]
                kept = gone + [m ^ 1 << bits[1] for m in gone]
            stay.append(kept)
        away = [[m | 1 << bits[0] for m in kept] for kept, bits in zip(stay, paths)]
        spots = [[order.index(m) for m in kept] for kept in away]
        sent = column_products(left, state["gated"], cut, spots, len(spots[0]))
        sent, left = yield (sent, left)
        got = [flip(values, bits[0] + 1) for values, bits in zip(sent, paths)]
        got = yield got
        if state["step"] == 1:
            got = lax.optimization_barrier((got, state["theirs"]))[0]
        spots = [[order.index(m) for m in kept] for kept in stay]
        gone = chips // 4
        if gone and j == len(cuts) - 1:
            moved = column_products(left, state["gated"], cut, [p[:gone] for p in spots], gone, got)
            got = [values[gone * cut :] for values in got]
            rest = column_products(left, state["gated"], cut, [p[gone:] for p in spots], 0, got)
        else:
            parts = column_products(left, state["gated"], cut, spots, gone, got)
            moved, rest = (parts[:2], parts[2:]) if gone else (None, parts)
        for step in range(1, len(chip_bits)):
            got, rest = yield ([flip(values, bits[step] + 1) for values, bits in zip(moved, paths)], rest)
            rest = [own + new.astype(f32) for own, new in zip(rest, got)]
            stay = [kept[len(kept) // 2 :] for kept in stay]
            if step + 1 < len(chip_bits):
                moved, after = [], []
                for total, kept, bits in zip(rest, stay, paths):
                    place = {m: total[i * cut : (i + 1) * cut] for i, m in enumerate(kept)}
                    gone = [m for m in kept if m >> bits[step + 1] & 1]
                    moved.append(jnp.concatenate([place[m].astype(bf16) for m in gone], axis=0))
                    after.append([place[m ^ 1 << bits[step + 1]] for m in gone])
                    kept[:] = gone + [m ^ 1 << bits[step + 1] for m in gone]
                rest = [jnp.concatenate(values, axis=0) for values in after]
        state["weight"] = lax.dynamic_update_slice(
            state["weight"], jnp.concatenate(rest, axis=1), (start, 0)
        )

    state["terms"] = []

    def rows_of_pre():
        weight_blocks = out_weight.reshape(shards, own_outs, width)

        def term(j):
            return (state["terms"][j], weight_blocks, *cuts[j])

        total = None
        for j in range(len(cuts) - 1):
            while len(state["terms"]) <= j:
                yield ()
            for _ in range(2 if j == 0 else 3):
                state["terms"][j] = yield state["terms"][j]
            (total,) = yield add_products(total, [term(j)])
        while len(state["terms"]) < len(cuts) or "adapter_terms" not in state:
            yield ()
        total, state["terms"][-1] = yield (total, state["terms"][-1])
        late = [term(len(cuts) - 1)] + state["adapter_terms"]
        hidden_grad, gate_part = yield add_products(total, late, (gate, hidden))
        gate_sum = jnp.where(live, gate_part[:, 0], 0.0)
        step = 1
        while step < planes:
            pairs = [(i, i ^ step) for i in range(planes)]
            gate_sum = gate_sum + lax.ppermute(gate_sum, "tp", pairs)
            step *= 2
        state["rows"] = (hidden_grad, gate_sum)

    def adapters():
        parts = [adapter_down.T[None], adapter_up[None]]
        paths = [chip_bits, chip_bits[::-1]]
        for step in range(len(chip_bits)):
            got = yield [flip(part, bits[step]) for part, bits in zip(parts, paths)]
            parts = [jnp.concatenate(two, axis=0) for two in zip(parts, got)]
        splits = rank // rank_rows

        def wide(values, part):
            return lax.dot_general(
                values, part.reshape(-1, width), contract_last, preferred_element_type=f32
            )

        sources = (hidden, cotangent)
        got = [flip(part, 0) for part in parts]
        first = [wide(values, part) for values, part in zip(sources, parts)]
        second = [wide(values, part) for values, part in zip(sources, got)]
        got, first, second = yield (got, first, second)
        blocks, products = [], []
        for i, bits in enumerate(paths):
            masks = masks_of(bits)
            others = [m ^ 1 for m in masks]
            blocks.append([(parts[i], masks), (got[i], others)])
            products.append([(first[i], masks), (second[i], others)])

        def select(products):
            out = [0.0] * splits
            for product, masks in products:
                for i, mask in enumerate(masks):
                    device = me ^ mask
                    here = depth == (device // splits + 1).astype(f32)
                    block = product[:, i * rank_rows : (i + 1) * rank_rows]
                    for h in range(splits):
                        out[h] += jnp.where((here & (device % splits == h))[:, None], block, 0.0)
            return out

        part = jnp.concatenate(select(products[0]) + select(products[1]), axis=1)
        part, blocks = yield (part, blocks[0])
        below = above = jnp.zeros_like(part)
        while state["step"] not in (0, min(2, planes - 1)):
            part = yield part
        for k in range(1, planes):
            sent = part + jnp.where(plane == k - 1, below, above)
            got = lax.ppermute(
                sent.astype(bf16), "tp", [(k - 1, k), (planes - k, planes - k - 1)]
            )
            if k == planes - 2 and state["step"]:
                state["hold"] = True
            got = yield got
            below = below + jnp.where(plane == k, got.astype(f32), 0.0)
            above = above + jnp.where(plane == planes - k - 1, got.astype(f32), 0.0)
        summed = part + below + above
        down, up = summed[:, :rank], adapter_scale * summed[:, rank:]

        def spread(masks):
            out = []
            for mask in masks:
                device = me ^ mask
                here = depth == (device // splits + 1).astype(f32)
                block = lax.dynamic_slice_in_dim(up, device % splits * rank_rows, rank_rows, axis=1)
                out.append(jnp.where(here[:, None], block, 0.0).astype(bf16))
            return jnp.concatenate(out, axis=1)

        state["adapter_terms"] = [
            (spread(masks), gathered, 0, rank_rows) for gathered, masks in blocks
        ]
        grads = jnp.concatenate(
            [gate[:, None] * up, gate[:, None] * adapter_scale * down], axis=1
        ).astype(bf16)
        other_grads = flip(grads, 0)
        other_hidden, other_dy, other_depth = state["other"]

        def rank_columns(values, depths):
            parts = []
            for m in order:
                start = ((chip ^ m) * 2 + core) * rank_rows
                part = lax.dynamic_slice_in_dim(values, start % rank, rank_rows, axis=1)
                here = depths == (start // rank + 1).astype(f32)
                parts.append(jnp.where(here[:, None], part, jnp.zeros((), bf16)))
            return jnp.concatenate(parts, axis=1)

        jobs = []
        for at, own, other, bits in (
            (0, hidden, other_hidden, chip_bits),
            (rank, cotangent, other_dy, chip_bits[::-1]),
        ):
            pairs = [
                (rank_columns(grads[:, at : at + rank], depth), own),
                (rank_columns(other_grads[:, at : at + rank], other_depth), other),
            ]
            jobs.append((pairs, bits))
        state["adapter_grads"] = yield from scatter(jobs, rank_rows)

    count = range(len(cuts))
    run(
        [line(), weights(), adapters()]
        + [weight_chunk(j) for j in reversed(range(len(cuts)))]
        + [rows_of_pre()]
    )
    hidden_grad, gate_grad = state["rows"]
    down_grad, up_grad = state["adapter_grads"]
    return (hidden_grad, gate_grad, state["weight"], down_grad, up_grad)


def solution(mesh):
    in_specs = (
        P("seq", "tp"),
        P("seq", "tp"),
        P("seq"),
        P("seq"),
        P(),
        P(None, "tp"),
        P("tp", "seq"),
        P("seq", "tp"),
    )
    out_specs = (P("seq", "tp"), P("seq"), P("seq", "tp"), P("seq", "tp"), P("seq", "tp"))
    return jax.shard_map(local, mesh=mesh, in_specs=in_specs, out_specs=out_specs, check_vma=False)
```
